768 devices in a mesh: blk: 64 (over y, x, core), grp: 12 (over z).
Axes of the slice: x: 4, y: 8, z: 12, core: 2. Of those that a mesh axis runs over, the one named last changes fastest.
Arguments:
- image_feats: bfloat16 [12288, 1536], P(('blk', 'grp')), may hold values from -6 to 6
- text_feats: bfloat16 [12288, 1024], P(('blk', 'grp')), may hold values from -6 to 6
- image_proj: bfloat16 [1536, 1152], replicated, may hold values from -0.15625 to 0.15625
- text_proj: bfloat16 [1024, 1152], replicated, may hold values from -0.1875 to 0.1875
- log_temp: float32 [1], replicated, may hold values from 4 to 4.8
- logit_bias: float32 [1], replicated, may hold values from -4 to -1
Outputs:
- image_grad: float32 [12288, 1536], P(('blk', 'grp'))
- text_grad: float32 [12288, 1024], P(('blk', 'grp'))
The draws below stay inside these ranges and needn't reach their ends.
All inputs are finite; a program needn't handle non-finite values.
Results may differ from the reference program's by a relative error of at most 0.0085.
Values may be sent and summed in bfloat16 or wider, within the bound.
No kernel may reach another device: no remote copies, remote signals or barrier semaphores. Data moves between devices by JAX's collectives and lax.ppermute only.
A program may use at most 64 MiB of HBM per device.

```python
import jax
import jax.numpy as jnp
from jax import lax

IMG_W = 1536
TXT_W = 1024
EMB = 1152
TOK_DEV = 16
BATCH = 12288
N_GRP = 12


def level_of(key, dims, cuts, low, top_value):
    def one(position, parts):
        heights = jax.random.uniform(jax.random.fold_in(jax.random.fold_in(key, 6), position), (parts,), jnp.float32, low / len(cuts), top_value / len(cuts))
        return jnp.repeat(jnp.exp(heights), dims[position] // parts).reshape((-1,) + (1,) * (len(dims) - position - 1))

    factor_of = one(*cuts[0])
    for cut in cuts[1:]:
        factor_of = factor_of * one(*cut)
    return factor_of


def normal_values(stream_key, dims, width, limit, shards=(), kind=jnp.bfloat16):
    gain = level_of(stream_key, dims, shards, -0.22, 0.18) if shards else 1.0
    result = jax.random.normal(stream_key, dims, jnp.float32) * width * gain
    return jnp.minimum(jnp.maximum(result, -limit), limit).astype(kind)


def setup_inputs(seed: int = 0) -> dict:
    key_of = jax.random.split(jax.random.key(seed), 7)
    image_feats = normal_values(key_of[0], (BATCH, IMG_W), 1.0, 6.0, ((0, 768),))
    text_feats = normal_values(key_of[1], (BATCH, TXT_W), 1.0, 6.0, ((0, 768),))
    image_proj = normal_values(key_of[2], (IMG_W, EMB), IMG_W ** -0.5, 0.15625)
    text_proj = normal_values(key_of[3], (TXT_W, EMB), TXT_W ** -0.5, 0.1875)
    log_temp = jnp.clip(jax.random.uniform(key_of[4], (1,), jnp.float32, 4.0, 4.8), 4.0, 4.8)
    logit_bias = jnp.clip(jax.random.uniform(key_of[5], (1,), jnp.float32, -4.0, -1.0), -4.0, -1.0)
    return dict(image_feats=image_feats, text_feats=text_feats, image_proj=image_proj, text_proj=text_proj, log_temp=log_temp, logit_bias=logit_bias)


loss_scale = 65536.0
eps = 1e-06

def embed(feats, proj):
    emb = jnp.dot(feats, proj, preferred_element_type=jnp.float32)
    inv = lax.rsqrt(lax.optimization_barrier(jnp.sum(emb * emb, axis=1, keepdims=True)) + eps)
    return (emb * inv, inv)

def backprop(unit, inv, grad_unit, proj):
    delta = inv * (grad_unit - unit * lax.optimization_barrier(jnp.sum(unit * grad_unit, axis=1, keepdims=True)))
    return jnp.dot(delta.astype(jnp.bfloat16), proj.T, preferred_element_type=jnp.float32)

def reference(image_feats, text_feats, image_proj, text_proj, log_temp, logit_bias):
    img_unit, img_inv = embed(image_feats, image_proj)
    txt_unit, txt_inv = embed(text_feats, text_proj)
    img_rows = img_unit.astype(jnp.bfloat16)
    txt_rows = txt_unit.astype(jnp.bfloat16)
    total = img_rows.shape[0]
    rows = TOK_DEV * N_GRP
    temp = jnp.exp(log_temp[0])
    bias = logit_bias[0]
    factor = loss_scale / total * temp
    columns = jnp.arange(total, dtype=jnp.int32)

    def block_step(text_acc, index):
        block = lax.dynamic_slice_in_dim(img_rows, index * rows, rows, 0)
        logits = jnp.dot(block, txt_rows.T, preferred_element_type=jnp.float32) * temp + bias
        row_ids = index * rows + jnp.arange(rows, dtype=jnp.int32)
        diag = (row_ids[:, None] == columns[None, :]).astype(jnp.float32)
        coef = (factor * (jax.nn.sigmoid(logits) - diag)).astype(jnp.bfloat16)
        img_du = jnp.dot(coef, txt_rows, preferred_element_type=jnp.float32)
        text_acc = text_acc + jnp.dot(coef.T, block, preferred_element_type=jnp.float32)
        return (text_acc, img_du)
    start = jnp.zeros((total, txt_rows.shape[1]), jnp.float32)
    txt_du, img_parts = lax.scan(block_step, start, jnp.arange(total // rows, dtype=jnp.int32))
    img_du = img_parts.reshape(total, txt_rows.shape[1])
    image_grad = backprop(img_unit, img_inv, img_du, image_proj)
    text_grad = backprop(txt_unit, txt_inv, txt_du, text_proj)
    return (image_grad, text_grad)
```

```python
import functools

import jax
import jax.numpy as jnp
import numpy as np
from jax import lax
from jax.experimental import pallas as pl
from jax.experimental.pallas import tpu as pltpu
from jax.sharding import Mesh
from jax.sharding import PartitionSpec as P

loss_scale = 65536.0
eps = 1e-06
f32 = jnp.float32
bf16 = jnp.bfloat16


def gathered(rows, axis):
    n = lax.axis_size(axis)
    copies = jnp.broadcast_to(rows[None], (n,) + rows.shape)
    return lax.all_to_all(copies, axis, 0, 0, tiled=True).reshape((-1,) + rows.shape[1:])


def scattered(parts, axis):
    n = lax.axis_size(axis)
    cut = parts.astype(bf16).reshape((n, -1) + parts.shape[1:])
    return jnp.sum(lax.all_to_all(cut, axis, 0, 0, tiled=True).astype(f32), axis=0)


def embed(feats, proj):
    emb = jnp.dot(feats, proj, preferred_element_type=f32)
    inv = lax.rsqrt(jnp.sum(emb * emb, axis=1, keepdims=True) + eps)
    return (emb * inv, inv)


def backprop(unit, inv, grad_unit, proj):
    delta = inv * (grad_unit - unit * jnp.sum(unit * grad_unit, axis=1, keepdims=True))
    return jnp.dot(delta.astype(bf16), proj.T, preferred_element_type=f32)


def tile_kernel(own, first, scalars, img_ref, txt_ref, img_out, txt_out):
    temp = scalars[0]
    bias = scalars[1]
    factor = scalars[2]
    img = img_ref[...]
    txt = txt_ref[...]
    logits = (
        lax.dot_general(img, txt, (((1,), (1,)), ((), ())), preferred_element_type=f32) * temp + bias
    )
    rows = lax.broadcasted_iota(jnp.int32, logits.shape, 0) - first[0]
    cols = lax.broadcasted_iota(jnp.int32, logits.shape, 1) - first[1]
    diag = ((rows == cols) & (rows >= 0) & (rows < own)).astype(f32)
    coef = (factor * (jax.nn.sigmoid(logits) - diag)).astype(bf16)
    img_out[...] = jnp.dot(coef, txt, preferred_element_type=f32).astype(img_out.dtype)
    txt_out[...] = lax.dot_general(
        coef, img, (((0,), (0,)), ((), ())), preferred_element_type=f32
    ).astype(txt_out.dtype)


def tile(own, first, scalars, img, txt):
    vmem = pl.BlockSpec(memory_space=pltpu.VMEM)
    smem = pl.BlockSpec(memory_space=pltpu.SMEM)
    n, m, w = img.shape[0], txt.shape[0], img.shape[1]
    return pl.pallas_call(
        functools.partial(tile_kernel, own),
        out_shape=[jax.ShapeDtypeStruct(img.shape, bf16), jax.ShapeDtypeStruct(txt.shape, bf16)],
        in_specs=[smem, smem, vmem, vmem],
        out_specs=[vmem, vmem],
        cost_estimate=pl.CostEstimate(
            flops=6 * n * m * w, bytes_accessed=4 * (n + m) * w, transcendentals=n * m
        ),
        compiler_params=pltpu.CompilerParams(vmem_limit_bytes=32 * 2**20),
    )(first, scalars, img, txt)


def shards(image_feats, text_feats, image_proj, text_proj, log_temp, logit_bias):
    own = text_feats.shape[0]
    total = own * lax.axis_size(("y", "x", "core", "z"))
    img_unit, img_inv = embed(image_feats, image_proj)
    txt_unit, txt_inv = embed(text_feats, text_proj)
    img_rows = lax.all_gather(gathered(img_unit.astype(bf16), "z"), "core", tiled=True)
    txt_rows = gathered(gathered(txt_unit.astype(bf16), "y"), "x")
    temp = jnp.exp(log_temp[0])
    scalars = jnp.stack([temp, logit_bias[0], loss_scale / total * temp])
    first = own * jnp.stack([lax.axis_index(("core", "z")), lax.axis_index(("x", "y"))])
    img_terms, txt_terms = tile(own, first, scalars, img_rows, txt_rows)
    img_du = scattered(scattered(img_terms, "core"), "z")
    txt_du = scattered(scattered(txt_terms, "x"), "y")
    image_grad = backprop(img_unit, img_inv, img_du, image_proj)
    text_grad = backprop(txt_unit, txt_inv, txt_du, text_proj)
    return (image_grad, text_grad)


def solution(mesh):
    blk, grp = mesh.devices.shape
    sizes = (blk // 8, 4, 2, grp)
    fine = Mesh(np.asarray(mesh.devices).reshape(sizes), ("y", "x", "core", "z"))
    rows = P(("y", "x", "core", "z"), None)
    return jax.shard_map(
        shards,
        mesh=fine,
        in_specs=(rows, rows, P(), P(), P(), P()),
        out_specs=(rows, rows),
        check_vma=False,
    )
```

```python
import functools

import jax
import jax.numpy as jnp
import numpy as np
from jax import lax
from jax.experimental import pallas as pl
from jax.experimental.pallas import tpu as pltpu
from jax.sharding import Mesh
from jax.sharding import PartitionSpec as P

loss_scale = 65536.0
eps = 1e-06
f32 = jnp.float32
bf16 = jnp.bfloat16


def shift(axis, by):
    n = lax.axis_size(axis)
    return [(i, (i + by) % n) for i in range(n)]


def gathered(rows, axis):
    n = lax.axis_size(axis)
    copies = jnp.broadcast_to(rows[None], (n,) + rows.shape)
    return lax.all_to_all(copies, axis, 0, 0, tiled=True).reshape((-1,) + rows.shape[1:])


def scattered(parts, axis):
    n = lax.axis_size(axis)
    cut = parts.astype(bf16).reshape((n, -1) + parts.shape[1:])
    return jnp.sum(lax.all_to_all(cut, axis, 0, 0, tiled=True).astype(f32), axis=0)


ahead = (0, 4, 8, 2, 6, 10, 1, 5, 9, 3, 7, 11)
z_axes = ("z3", "z4")


def reduced_along_z(parts, own):
    for by in (1, 2):
        half = parts.shape[0] // 2
        got = lax.ppermute(parts[half:].astype(bf16), z_axes, shift(z_axes, by))
        parts = parts[:half] + got.astype(f32)
    far = [
        lax.ppermute(parts[k * own : (k + 1) * own].astype(bf16), z_axes, shift(z_axes, 4 * k))
        for k in (1, 2)
    ]
    return parts[:own] + far[0].astype(f32) + far[1].astype(f32)


def embed(feats, proj):
    emb = jnp.dot(feats, proj, preferred_element_type=f32)
    inv = lax.rsqrt(jnp.sum(emb * emb, axis=1, keepdims=True) + eps)
    return (emb * inv, inv)


def backprop(unit, inv, grad_unit, proj):
    delta = inv * (grad_unit - unit * jnp.sum(unit * grad_unit, axis=1, keepdims=True))
    return jnp.dot(delta.astype(bf16), proj.T, preferred_element_type=f32)


def tile_kernel(own, place, scalars, img_ref, txt_ref, near_out, far_out, txt_out, img_buf):
    temp = scalars[0]
    bias = scalars[1]
    factor = scalars[2]
    core = place[0]
    z = place[1]
    half = len(ahead) * own
    for c in range(2):
        for k, by in enumerate(ahead):
            owner = lax.rem(z + by, 12)
            block = lax.rem(core + c, 2) * 12 + lax.rem(owner, 4) * 3 + lax.div(owner, 4)
            img_buf[pl.ds(c * half + k * own, own), :] = img_ref[
                pl.ds(pl.multiple_of(block * own, own), own), :
            ]
    img = img_buf[...]
    txt = txt_ref[...]
    logits = (
        lax.dot_general(img, txt, (((1,), (1,)), ((), ())), preferred_element_type=f32) * temp + bias
    )
    rows = lax.broadcasted_iota(jnp.int32, logits.shape, 0)
    cols = lax.broadcasted_iota(jnp.int32, logits.shape, 1) - place[2]
    diag = ((rows == cols) & (rows < own)).astype(f32)
    coef = (factor * (jax.nn.sigmoid(logits) - diag)).astype(bf16)
    txt_out[...] = lax.dot_general(
        coef, img, (((0,), (0,)), ((), ())), preferred_element_type=f32
    ).astype(bf16)
    img_du = jnp.dot(coef, txt, preferred_element_type=f32)
    near_out[...] = img_du[:half]
    far_out[...] = img_du[half:].astype(bf16)


def tile(own, place, scalars, img, txt):
    vmem = pl.BlockSpec(memory_space=pltpu.VMEM)
    smem = pl.BlockSpec(memory_space=pltpu.SMEM)
    n, m, w = img.shape[0], txt.shape[0], img.shape[1]
    return pl.pallas_call(
        functools.partial(tile_kernel, own),
        out_shape=[
            jax.ShapeDtypeStruct((n // 2, w), f32),
            jax.ShapeDtypeStruct((n // 2, w), bf16),
            jax.ShapeDtypeStruct((m, w), bf16),
        ],
        in_specs=[smem, smem, vmem, vmem],
        out_specs=[vmem, vmem, vmem],
        scratch_shapes=[pltpu.VMEM((n, w), bf16)],
        cost_estimate=pl.CostEstimate(
            flops=6 * n * m * w, bytes_accessed=4 * (n + m) * w, transcendentals=n * m
        ),
        compiler_params=pltpu.CompilerParams(vmem_limit_bytes=32 * 2**20),
    )(place, scalars, img, txt)


def shards(image_feats, text_feats, image_proj, text_proj, log_temp, logit_bias):
    own = text_feats.shape[0]
    total = own * lax.axis_size(("y", "x", "core") + z_axes)
    img_unit, img_inv = embed(image_feats, image_proj)
    txt_unit, txt_inv = embed(text_feats, text_proj)
    img_rows = lax.all_gather(img_unit.astype(bf16), "z3", tiled=True)
    txt_rows = gathered(txt_unit.astype(bf16), "y")
    img_rows, txt_rows = lax.optimization_barrier((img_rows, txt_rows))
    img_rows = lax.all_gather(lax.all_gather(img_rows, "z4", tiled=True), "core", tiled=True)
    txt_rows = gathered(txt_rows, "x")
    temp = jnp.exp(log_temp[0])
    scalars = jnp.stack([temp, logit_bias[0], loss_scale / total * temp])
    place = jnp.stack(
        [lax.axis_index("core"), lax.axis_index(z_axes), own * lax.axis_index(("x", "y"))]
    )
    near, far, txt_terms = tile(own, place, scalars, img_rows, txt_rows)
    near = near + lax.ppermute(far, "core", shift("core", 1)).astype(f32)
    img_du = reduced_along_z(near, own)
    txt_du = scattered(scattered(txt_terms, "x"), "y")
    image_grad = backprop(img_unit, img_inv, img_du, image_proj)
    text_grad = backprop(txt_unit, txt_inv, txt_du, text_proj)
    return (image_grad, text_grad)


def solution(mesh):
    blk, grp = mesh.devices.shape
    sizes = (blk // 8, 4, 2, grp // 4, 4)
    fine = Mesh(np.asarray(mesh.devices).reshape(sizes), ("y", "x", "core") + z_axes)
    rows = P(("y", "x", "core") + z_axes, None)
    return jax.shard_map(
        shards,
        mesh=fine,
        in_specs=(rows, rows, P(), P(), P(), P()),
        out_specs=(rows, rows),
        check_vma=False,
    )
```

```python
import functools

import jax
import jax.numpy as jnp
import numpy as np
from jax import lax
from jax.experimental import pallas as pl
from jax.experimental.pallas import tpu as pltpu
from jax.sharding import Mesh
from jax.sharding import PartitionSpec as P

loss_scale = 65536.0
eps = 1e-06
f32 = jnp.float32
bf16 = jnp.bfloat16

vmem = pl.BlockSpec(memory_space=pltpu.VMEM)
smem = pl.BlockSpec(memory_space=pltpu.SMEM)
hbm = pl.BlockSpec(memory_space=pltpu.HBM)
params = pltpu.CompilerParams(vmem_limit_bytes=24 * 2**20)


def cost(flops, moved, transcendentals=0):
    return pl.CostEstimate(flops=flops, bytes_accessed=moved, transcendentals=transcendentals)


def shift(axis, by):
    n = lax.axis_size(axis)
    return [(i, (i + by) % n) for i in range(n)]


def exchanged(copies, axis):
    return lax.all_to_all(copies, axis, 0, 0, tiled=True)


def embed_kernel(feats, proj, unit_out, inv_out, rows_out, acc):
    step = pl.program_id(0)

    @pl.when(step == 0)
    def _():
        acc[...] = jnp.zeros_like(acc)

    acc[...] += jnp.dot(feats[...], proj[...], preferred_element_type=f32)

    @pl.when(step == pl.num_programs(0) - 1)
    def _():
        emb = acc[...]
        inv = lax.rsqrt(jnp.sum(emb * emb, axis=1, keepdims=True) + eps)
        unit = emb * inv
        unit_out[...] = unit
        inv_out[...] = jnp.broadcast_to(inv, inv_out.shape)
        rows_out[...] = unit.astype(bf16)


def embed(feats, proj):
    own, depth = feats.shape
    width = proj.shape[1]
    cut = 512
    whole = lambda shape: pl.BlockSpec(shape, lambda k: (0, 0))
    return pl.pallas_call(
        embed_kernel,
        grid=(depth // cut,),
        out_shape=[
            jax.ShapeDtypeStruct((own, width), f32),
            jax.ShapeDtypeStruct((own, 128), f32),
            jax.ShapeDtypeStruct((own, width), bf16),
        ],
        in_specs=[
            pl.BlockSpec((own, cut), lambda k: (0, k)),
            pl.BlockSpec((cut, width), lambda k: (k, 0)),
        ],
        out_specs=[whole((own, width)), whole((own, 128)), whole((own, width))],
        scratch_shapes=[pltpu.VMEM((own, width), f32)],
        cost_estimate=cost(2 * own * depth * width, 2 * depth * width),
        compiler_params=params,
    )(feats, proj)


def repeat_kernel(rows, out, sems):
    copies = [pltpu.make_async_copy(rows, out.at[k], sems.at[k]) for k in range(out.shape[0])]
    for copy in copies:
        copy.start()
    for copy in copies:
        copy.wait()


def repeated(rows, n):
    return pl.pallas_call(
        repeat_kernel,
        out_shape=jax.ShapeDtypeStruct((n,) + rows.shape, rows.dtype),
        in_specs=[vmem],
        out_specs=hbm,
        scratch_shapes=[pltpu.SemaphoreType.DMA((n,))],
        cost_estimate=cost(0, 4 * n * rows.size),
    )(rows)


def text_kernel(own, place, scalars, near, far, txt, txt_out, coef_out, img, buf, sems):
    temp = scalars[0]
    bias = scalars[1]
    factor = scalars[2]
    half = near.shape[0]
    img[:half] = near[...]
    img[half:] = far[...]
    rows = img[...]
    n = txt_out.shape[0]
    copies = []
    for q in range(n):
        size = txt_out.shape[1]
        part = slice(q * size, (q + 1) * size)
        logits = (
            lax.dot_general(
                txt[part], rows, (((1,), (1,)), ((), ())), preferred_element_type=f32
            )
            * temp
            + bias
        )
        txt_ids = lax.broadcasted_iota(jnp.int32, logits.shape, 0) + (q * size - place[0])
        img_ids = lax.broadcasted_iota(jnp.int32, logits.shape, 1)
        diag = ((txt_ids == img_ids) & (img_ids < own)).astype(f32)
        coef = (factor * (jax.nn.sigmoid(logits) - diag)).astype(bf16)
        coef_out[part] = coef
        buf[q] = jnp.dot(coef, rows, preferred_element_type=f32).astype(bf16)
        copies.append(pltpu.make_async_copy(buf.at[q], txt_out.at[q], sems.at[q]))
        copies[-1].start()
    for copy in copies:
        copy.wait()


def text_terms(own, place, scalars, near, far, txt, n):
    m, w = txt.shape
    i = 2 * near.shape[0]
    return pl.pallas_call(
        functools.partial(text_kernel, own),
        out_shape=[
            jax.ShapeDtypeStruct((n, m // n, w), bf16),
            jax.ShapeDtypeStruct((m, i), bf16),
        ],
        in_specs=[smem, smem, vmem, vmem, vmem],
        out_specs=[hbm, vmem],
        scratch_shapes=[
            pltpu.VMEM((i, w), bf16),
            pltpu.VMEM((n, m // n, w), bf16),
            pltpu.SemaphoreType.DMA((n,)),
        ],
        cost_estimate=cost(4 * i * m * w, 4 * (i + m) * w, i * m),
        compiler_params=params,
    )(place, scalars, near, far, txt)


def image_kernel(coef, txt, near_out, far_out):
    half = near_out.shape[0]
    terms = lax.dot_general(
        coef[...], txt[...], (((0,), (0,)), ((), ())), preferred_element_type=f32
    )
    near_out[...] = terms[:half]
    far_out[...] = terms[half:].astype(bf16)


def image_terms(coef, txt):
    m, i = coef.shape
    w = txt.shape[1]
    return pl.pallas_call(
        image_kernel,
        out_shape=[
            jax.ShapeDtypeStruct((i // 2, w), f32),
            jax.ShapeDtypeStruct((i // 2, w), bf16),
        ],
        in_specs=[vmem, vmem],
        out_specs=[vmem, vmem],
        cost_estimate=cost(2 * i * m * w, 4 * (i + m) * w),
        compiler_params=params,
    )(coef, txt)


def fold_kernel(parts, got, *outs):
    at = 0
    for out in outs:
        rows = slice(at, at + out.shape[0])
        out[...] = (parts[rows] + got[rows].astype(f32)).astype(out.dtype)
        at += out.shape[0]


def fold(parts, got, sends):
    n, w = parts.shape
    sizes = (n - sum(sends),) + tuple(sends)
    return pl.pallas_call(
        fold_kernel,
        out_shape=[
            jax.ShapeDtypeStruct((size, w), f32 if k == 0 else bf16)
            for k, size in enumerate(sizes)
        ],
        in_specs=[vmem, vmem],
        out_specs=[vmem] * len(sizes),
        cost_estimate=cost(n * w, 10 * n * w),
        compiler_params=params,
    )(parts, got)


def sum_kernel(parts, out, buf, sem):
    total = parts[0].astype(f32)
    for k in range(1, parts.shape[0]):
        total += parts[k].astype(f32)
    buf[...] = total.astype(bf16)
    copy = pltpu.make_async_copy(buf, out, sem)
    copy.start()
    copy.wait()


def summed(parts):
    n, m, w = parts.shape
    return pl.pallas_call(
        sum_kernel,
        out_shape=jax.ShapeDtypeStruct((m, w), bf16),
        in_specs=[vmem],
        out_specs=hbm,
        scratch_shapes=[pltpu.VMEM((m, w), bf16), pltpu.SemaphoreType.DMA],
        cost_estimate=cost(n * m * w, 2 * (n + 1) * m * w),
        compiler_params=params,
    )(parts)


def backprop_kernel(unit, inv, proj, *refs):
    *parts, out = refs
    total = 0.0
    for part in parts:
        if len(part.shape) == 2:
            total = total + part[...].astype(f32)
        else:
            for k in range(part.shape[0]):
                total = total + part[k].astype(f32)
    rows = unit[...]
    along = jnp.sum(rows * total, axis=1, keepdims=True)
    delta = (inv[:, :1] * (total - rows * along)).astype(bf16)
    out[...] = lax.dot_general(
        delta, proj[...], (((1,), (1,)), ((), ())), preferred_element_type=f32
    )


def backprop(unit, inv, proj, *parts):
    depth, width = proj.shape
    own = unit.shape[0]
    return pl.pallas_call(
        backprop_kernel,
        out_shape=jax.ShapeDtypeStruct((own, depth), f32),
        in_specs=[vmem] * (3 + len(parts)),
        out_specs=vmem,
        cost_estimate=cost(2 * own * depth * width, 2 * depth * width),
        compiler_params=params,
    )(unit, inv, proj, *parts)


def shards(image_feats, text_feats, image_proj, text_proj, log_temp, logit_bias):
    own = text_feats.shape[0]
    total = own * lax.axis_size(("y", "x", "core", "z"))
    nx, ny = lax.axis_size("x"), lax.axis_size("y")
    send = lambda rows, axis, by: lax.ppermute(rows, axis, shift(axis, by))

    txt_unit, txt_inv, txt_own = embed(text_feats, text_proj)
    img_unit, img_inv, img_own = embed(image_feats, image_proj)
    txt_rows = exchanged(jnp.broadcast_to(txt_own[None], (ny,) + txt_own.shape), "y")
    img_rows = jnp.concatenate([img_own, send(img_own, "z", -4), send(img_own, "z", -8)])
    img_rows, txt_rows = lax.optimization_barrier((img_rows, txt_rows))
    txt_rows = exchanged(repeated(txt_rows.reshape(ny * own, -1), nx), "x")
    txt_rows = txt_rows.reshape(nx * ny * own, -1)
    for by in (2, 1):
        img_rows = jnp.concatenate([img_rows, send(img_rows, "z", -by)])
    img_far = send(img_rows, "core", 1)

    temp = jnp.exp(log_temp[0])
    scalars = jnp.stack([temp, logit_bias[0], loss_scale / total * temp])
    place = jnp.reshape(own * lax.axis_index(("x", "y")), (1,))
    txt_terms, coef = text_terms(own, place, scalars, img_rows, img_far, txt_rows, nx)
    txt_terms = exchanged(txt_terms, "x")
    near, far = image_terms(coef, txt_rows)
    near, away = fold(near, send(far, "core", 1), (6 * own,))
    near, away = fold(near, send(away, "z", 1), (3 * own,))
    near, away4, away8 = fold(near, send(away, "z", 2), (own, own))
    txt_terms, near, away4, away8 = lax.optimization_barrier((txt_terms, near, away4, away8))
    txt_terms = exchanged(summed(txt_terms).reshape(ny, own, -1), "y")
    image_grad = backprop(
        img_unit, img_inv, image_proj, near, send(away4, "z", 4), send(away8, "z", 8)
    )
    text_grad = backprop(txt_unit, txt_inv, text_proj, txt_terms)
    return (image_grad, text_grad)


def solution(mesh):
    blk, grp = mesh.devices.shape
    fine = Mesh(np.asarray(mesh.devices).reshape(blk // 8, 4, 2, grp), ("y", "x", "core", "z"))
    rows = P(("y", "x", "core", "z"), None)
    return jax.shard_map(
        shards,
        mesh=fine,
        in_specs=(rows, rows, P(), P(), P(), P()),
        out_specs=(rows, rows),
        check_vma=False,
    )
```

```python
import functools

import jax
import jax.numpy as jnp
import numpy as np
from jax import lax
from jax.experimental import pallas as pl
from jax.experimental.pallas import tpu as pltpu
from jax.sharding import Mesh
from jax.sharding import PartitionSpec as P

loss_scale = 65536.0
eps = 1e-06
f32 = jnp.float32
bf16 = jnp.bfloat16

vmem = pl.BlockSpec(memory_space=pltpu.VMEM)
smem = pl.BlockSpec(memory_space=pltpu.SMEM)
hbm = pl.BlockSpec(memory_space=pltpu.HBM)
params = pltpu.CompilerParams(vmem_limit_bytes=24 * 2**20)

anywhere = pl.BlockSpec(memory_space=pl.ANY)

ahead = (0, 4, 8, 2, 6, 10, 1, 5, 9, 3, 7, 11)


def cost(flops, moved, transcendentals=0):
    return pl.CostEstimate(flops=flops, bytes_accessed=moved, transcendentals=transcendentals)


def shift(axis, by):
    n = lax.axis_size(axis)
    return [(i, (i + by) % n) for i in range(n)]


def exchanged(copies, axis):
    return lax.all_to_all(copies, axis, 0, 0, tiled=True)


def embed_kernel(feats, proj, unit_out, inv_out, rows_out, feats_buf, proj_buf, unit_buf, rows_buf, sems, out_sems):
    parts, cut = proj_buf.shape[:2]
    reads = [pltpu.make_async_copy(feats, feats_buf, sems.at[parts])]
    for k in range(parts):
        reads.append(pltpu.make_async_copy(proj.at[pl.ds(k * cut, cut)], proj_buf.at[k], sems.at[k]))
    for read in reads:
        read.start()
    reads[0].wait()
    emb = jnp.zeros(unit_buf.shape, f32)
    for k in range(parts):
        reads[k + 1].wait()
        emb += jnp.dot(
            feats_buf[:, k * cut : (k + 1) * cut], proj_buf[k], preferred_element_type=f32
        )
    inv = lax.rsqrt(jnp.sum(emb * emb, axis=1, keepdims=True) + eps)
    unit = emb * inv
    rows_buf[...] = unit.astype(bf16)
    n = rows_out.shape[0]
    writes = [pltpu.make_async_copy(rows_buf, rows_out.at[k], out_sems.at[k]) for k in range(n)]
    for write in writes:
        write.start()
    unit_buf[...] = unit
    writes.append(pltpu.make_async_copy(unit_buf, unit_out, out_sems.at[n]))
    writes[-1].start()
    inv_out[...] = jnp.broadcast_to(inv, inv_out.shape)
    for write in writes:
        write.wait()


def embed(feats, proj, n):
    own, depth = feats.shape
    width = proj.shape[1]
    cut = 256
    return pl.pallas_call(
        embed_kernel,
        out_shape=[
            jax.ShapeDtypeStruct((own, width), f32),
            jax.ShapeDtypeStruct((own, 128), f32),
            jax.ShapeDtypeStruct((n, own, width), bf16),
        ],
        in_specs=[anywhere, anywhere],
        out_specs=[hbm, vmem, hbm],
        scratch_shapes=[
            pltpu.VMEM((own, depth), bf16),
            pltpu.VMEM((depth // cut, cut, width), bf16),
            pltpu.VMEM((own, width), f32),
            pltpu.VMEM((own, width), bf16),
            pltpu.SemaphoreType.DMA((depth // cut + 1,)),
            pltpu.SemaphoreType.DMA((n + 1,)),
        ],
        cost_estimate=cost(2 * own * depth * width, 2 * depth * width),
        compiler_params=params,
    )(feats, proj)


def text_kernel(own, place, scalars, img, txt, txt_out, coef_out, buf, sems):
    temp = scalars[0]
    bias = scalars[1]
    factor = scalars[2]
    rows = img[...]
    parts, size = buf.shape[:2]
    copies = []
    for q in range(parts):
        part = slice(q * size, (q + 1) * size)
        logits = (
            lax.dot_general(
                txt[part], rows, (((1,), (1,)), ((), ())), preferred_element_type=f32
            )
            * temp
            + bias
        )
        txt_ids = lax.broadcasted_iota(jnp.int32, logits.shape, 0) + (q * size - place[0])
        img_ids = lax.broadcasted_iota(jnp.int32, logits.shape, 1) - place[1]
        diag = ((txt_ids == img_ids) & (img_ids >= 0) & (img_ids < own)).astype(f32)
        coef = (factor * (jax.nn.sigmoid(logits) - diag)).astype(bf16)
        coef_out[part] = coef
        buf[q] = jnp.dot(coef, rows, preferred_element_type=f32).astype(bf16)
        copies.append(
            pltpu.make_async_copy(buf.at[q], txt_out.at[pl.ds(q * size, size)], sems.at[q])
        )
        copies[-1].start()
    for copy in copies:
        copy.wait()


def text_terms(own, place, scalars, img, txt):
    m, w = txt.shape
    i = img.shape[0]
    parts = 4
    return pl.pallas_call(
        functools.partial(text_kernel, own),
        out_shape=[jax.ShapeDtypeStruct((m, w), bf16), jax.ShapeDtypeStruct((m, i), bf16)],
        in_specs=[smem, smem, vmem, vmem],
        out_specs=[hbm, vmem],
        scratch_shapes=[
            pltpu.VMEM((parts, m // parts, w), bf16),
            pltpu.SemaphoreType.DMA((parts,)),
        ],
        cost_estimate=cost(4 * i * m * w, 4 * (i + m) * w, i * m),
        compiler_params=params,
    )(place, scalars, img, txt)


def image_kernel(own, place, coef, txt, near_out, far_out, terms):
    nz = len(ahead)
    half = nz * own
    terms[...] = lax.dot_general(
        coef[...], txt[...], (((0,), (0,)), ((), ())), preferred_element_type=f32
    )
    core = place[2]
    z = place[3]
    for k, by in enumerate(ahead):
        owner = lax.rem(z + by, nz) * own
        near = pl.multiple_of(core * half + owner, own)
        far = pl.multiple_of((1 - core) * half + owner, own)
        near_out[pl.ds(k * own, own)] = terms[pl.ds(near, own)]
        far_out[pl.ds(k * own, own)] = terms[pl.ds(far, own)].astype(bf16)


def image_terms(own, place, coef, txt):
    m, i = coef.shape
    w = txt.shape[1]
    return pl.pallas_call(
        functools.partial(image_kernel, own),
        out_shape=[
            jax.ShapeDtypeStruct((i // 2, w), f32),
            jax.ShapeDtypeStruct((i // 2, w), bf16),
        ],
        in_specs=[smem, vmem, vmem],
        out_specs=[vmem, vmem],
        scratch_shapes=[pltpu.VMEM((i, w), f32)],
        cost_estimate=cost(2 * i * m * w, 4 * (i + m) * w),
        compiler_params=params,
    )(place, coef, txt)


def fold_kernel(parts, got, *outs):
    at = 0
    for out in outs:
        rows = slice(at, at + out.shape[0])
        out[...] = (parts[rows] + got[rows].astype(f32)).astype(out.dtype)
        at += out.shape[0]


def fold(parts, got, sends):
    n, w = parts.shape
    sizes = (n - sum(sends),) + tuple(sends)
    return pl.pallas_call(
        fold_kernel,
        out_shape=[
            jax.ShapeDtypeStruct((size, w), f32 if k == 0 else bf16)
            for k, size in enumerate(sizes)
        ],
        in_specs=[vmem, vmem],
        out_specs=[vmem] * len(sizes),
        cost_estimate=cost(n * w, 10 * n * w),
        compiler_params=params,
    )(parts, got)


def backprop_kernel(unit, inv, proj, *refs):
    *parts, out, unit_buf, proj_buf, sems = refs
    reads = [
        pltpu.make_async_copy(unit, unit_buf, sems.at[0]),
        pltpu.make_async_copy(proj, proj_buf, sems.at[1]),
    ]
    for read in reads:
        read.start()
    total = 0.0
    for part in parts:
        if len(part.shape) == 2:
            total = total + part[...].astype(f32)
        else:
            for k in range(part.shape[0]):
                total = total + part[k].astype(f32)
    reads[0].wait()
    rows = unit_buf[...]
    along = jnp.sum(rows * total, axis=1, keepdims=True)
    delta = (inv[:, :1] * (total - rows * along)).astype(bf16)
    reads[1].wait()
    out[...] = lax.dot_general(
        delta, proj_buf[...], (((1,), (1,)), ((), ())), preferred_element_type=f32
    )


def backprop(unit, inv, proj, *parts):
    depth, width = proj.shape
    own = unit.shape[0]
    return pl.pallas_call(
        backprop_kernel,
        out_shape=jax.ShapeDtypeStruct((own, depth), f32),
        in_specs=[anywhere, vmem, anywhere] + [vmem] * len(parts),
        out_specs=vmem,
        scratch_shapes=[
            pltpu.VMEM(unit.shape, f32),
            pltpu.VMEM(proj.shape, bf16),
            pltpu.SemaphoreType.DMA((2,)),
        ],
        cost_estimate=cost(2 * own * depth * width, 2 * depth * width),
        compiler_params=params,
    )(unit, inv, proj, *parts)


def shards(image_feats, text_feats, image_proj, text_proj, log_temp, logit_bias):
    own = text_feats.shape[0]
    total = own * lax.axis_size(("y", "x", "core", "z"))
    send = lambda rows, axis, by: lax.ppermute(rows, axis, shift(axis, by))

    txt_unit, txt_inv, txt_rows = embed(text_feats, text_proj, lax.axis_size(("y", "x")))
    txt_rows = exchanged(txt_rows, ("y", "x")).reshape(-1, txt_rows.shape[2])
    img_unit, img_inv, img_rows = embed(image_feats, image_proj, 1)
    img_rows = lax.all_gather(img_rows[0], "z", tiled=True)
    img_rows = lax.all_gather(img_rows, "core", tiled=True)

    temp = jnp.exp(log_temp[0])
    scalars = jnp.stack([temp, logit_bias[0], loss_scale / total * temp])
    core, z = lax.axis_index("core"), lax.axis_index("z")
    place = jnp.stack(
        [own * lax.axis_index(("y", "x")), own * lax.axis_index(("core", "z")), core, z]
    )
    txt_terms, coef = text_terms(own, place, scalars, img_rows, txt_rows)
    txt_terms = exchanged(txt_terms.reshape(-1, own, txt_terms.shape[1]), ("y", "x"))
    near, far = image_terms(own, place, coef, txt_rows)
    near, away = fold(near, send(far, "core", 1), (6 * own,))
    near, away = fold(near, send(away, "z", 1), (3 * own,))
    near, away4, away8 = fold(near, send(away, "z", 2), (own, own))
    image_grad = backprop(
        img_unit, img_inv, image_proj, near, send(away4, "z", 4), send(away8, "z", 8)
    )
    text_grad = backprop(txt_unit, txt_inv, text_proj, txt_terms)
    return (image_grad, text_grad)


def solution(mesh):
    blk, grp = mesh.devices.shape
    fine = Mesh(np.asarray(mesh.devices).reshape(blk // 8, 4, 2, grp), ("y", "x", "core", "z"))
    rows = P(("y", "x", "core", "z"), None)
    return jax.shard_map(
        shards,
        mesh=fine,
        in_specs=(rows, rows, P(), P(), P(), P()),
        out_specs=(rows, rows),
        check_vma=False,
    )
```

```python
import functools

import jax
import jax.numpy as jnp
import numpy as np
from jax import lax
from jax.experimental import pallas as pl
from jax.experimental.pallas import tpu as pltpu
from jax.sharding import Mesh
from jax.sharding import PartitionSpec as P

loss_scale = 65536.0
eps = 1e-06
f32 = jnp.float32
bf16 = jnp.bfloat16

vmem = pl.BlockSpec(memory_space=pltpu.VMEM)
smem = pl.BlockSpec(memory_space=pltpu.SMEM)
hbm = pl.BlockSpec(memory_space=pltpu.HBM)
params = pltpu.CompilerParams(vmem_limit_bytes=24 * 2**20)


def far_off(x):
    return pltpu.with_memory_space_constraint(x, pltpu.HBM)

ahead = (0, 4, 8, 1, 5, 9, 2, 6, 10, 11, 3, 7)


def cost(flops, moved, transcendentals=0):
    return pl.CostEstimate(flops=flops, bytes_accessed=moved, transcendentals=transcendentals)


def shift(axis, by):
    n = lax.axis_size(axis)
    return [(i, (i + by) % n) for i in range(n)]


def exchanged(copies, axis):
    return lax.all_to_all(copies, axis, 0, 0, tiled=True)


def embed_kernel(feats, proj, unit_out, inv_out, rows_out, feats_buf, proj_buf, unit_buf, rows_buf, sems, out_sems):
    parts, cut = proj_buf.shape[:2]
    reads = [pltpu.make_async_copy(feats, feats_buf, sems.at[parts])]
    for k in range(parts):
        reads.append(pltpu.make_async_copy(proj.at[pl.ds(k * cut, cut)], proj_buf.at[k], sems.at[k]))
    for read in reads:
        read.start()
    reads[0].wait()
    emb = jnp.zeros(unit_buf.shape, f32)
    for k in range(parts):
        reads[k + 1].wait()
        emb += jnp.dot(
            feats_buf[:, k * cut : (k + 1) * cut], proj_buf[k], preferred_element_type=f32
        )
    inv = lax.rsqrt(jnp.sum(emb * emb, axis=1, keepdims=True) + eps)
    unit = emb * inv
    rows_buf[...] = unit.astype(bf16)
    n = rows_out.shape[0]
    writes = [pltpu.make_async_copy(rows_buf, rows_out.at[k], out_sems.at[k]) for k in range(n)]
    for write in writes:
        write.start()
    unit_buf[...] = unit
    writes.append(pltpu.make_async_copy(unit_buf, unit_out, out_sems.at[n]))
    writes[-1].start()
    inv_out[...] = jnp.broadcast_to(inv, inv_out.shape)
    for write in writes:
        write.wait()


def embed(feats, proj, n):
    own, depth = feats.shape
    width = proj.shape[1]
    cut = 256
    return pl.pallas_call(
        embed_kernel,
        out_shape=[
            pltpu.HBM((own, width), f32),
            jax.ShapeDtypeStruct((own, 128), f32),
            pltpu.HBM((n, own, width), bf16),
        ],
        in_specs=[hbm, hbm],
        out_specs=[hbm, vmem, hbm],
        scratch_shapes=[
            pltpu.VMEM((own, depth), bf16),
            pltpu.VMEM((depth // cut, cut, width), bf16),
            pltpu.VMEM((own, width), f32),
            pltpu.VMEM((own, width), bf16),
            pltpu.SemaphoreType.DMA((depth // cut + 1,)),
            pltpu.SemaphoreType.DMA((n + 1,)),
        ],
        cost_estimate=cost(2 * own * depth * width, 2 * depth * width),
        compiler_params=params,
    )(far_off(feats), far_off(proj))


def image_kernel(own, factor, log_temp, bias, img, txt, coef_out, near_out, far_out, terms):
    nz = len(ahead)
    core = lax.axis_index("core")
    z = lax.axis_index("z")
    first_img = (core * nz + z) * own
    first_txt = lax.axis_index(("y", "x")) * own
    temp = jnp.exp(jnp.full((1, img.shape[0]), log_temp[0], f32))
    factor = factor * temp
    rows = img[...]
    size = 256
    total = 0.0
    for at in range(0, txt.shape[0], size):
        part = slice(at, at + size)
        logits = (
            lax.dot_general(
                txt[part], rows, (((1,), (1,)), ((), ())), preferred_element_type=f32
            )
            * temp
            + bias[0]
        )
        txt_ids = lax.broadcasted_iota(jnp.int32, logits.shape, 0) + (at - first_txt)
        img_ids = lax.broadcasted_iota(jnp.int32, logits.shape, 1) - first_img
        diag = ((txt_ids == img_ids) & (img_ids >= 0) & (img_ids < own)).astype(f32)
        coef = (factor * (jax.nn.sigmoid(logits) - diag)).astype(bf16)
        coef_out[part] = coef
        total = total + lax.dot_general(
            coef, txt[part], (((0,), (0,)), ((), ())), preferred_element_type=f32
        )
    terms[...] = total
    half = nz * own
    for k, by in enumerate(ahead):
        owner = lax.rem(z + by, nz) * own
        near = pl.multiple_of(core * half + owner, own)
        far = pl.multiple_of((1 - core) * half + owner, own)
        near_out[pl.ds(k * own, own)] = terms[pl.ds(near, own)]
        far_out[pl.ds(k * own, own)] = terms[pl.ds(far, own)].astype(bf16)


def image_terms(own, log_temp, bias, factor, img, txt):
    m, w = txt.shape
    i = img.shape[0]
    return pl.pallas_call(
        functools.partial(image_kernel, own, factor),
        out_shape=[
            jax.ShapeDtypeStruct((m, i), bf16),
            jax.ShapeDtypeStruct((i // 2, w), f32),
            jax.ShapeDtypeStruct((i // 2, w), bf16),
        ],
        in_specs=[smem, smem, vmem, vmem],
        out_specs=[vmem, vmem, vmem],
        scratch_shapes=[pltpu.VMEM((i, w), f32)],
        cost_estimate=cost(4 * i * m * w, 4 * (i + m) * w, i * m),
        compiler_params=params,
    )(log_temp, bias, img, txt)


def text_kernel(coef, img, out, buf, sems):
    rows = img[...]
    parts, size = buf.shape[:2]
    writes = []
    for q in range(parts):
        buf[q] = jnp.dot(
            coef[q * size : (q + 1) * size], rows, preferred_element_type=f32
        ).astype(bf16)
        writes.append(pltpu.make_async_copy(buf.at[q], out.at[pl.ds(q * size, size)], sems.at[q]))
        writes[-1].start()
    for write in writes:
        write.wait()


def text_terms(coef, img):
    m, i = coef.shape
    w = img.shape[1]
    parts = 2
    return pl.pallas_call(
        text_kernel,
        out_shape=pltpu.HBM((m, w), bf16),
        in_specs=[vmem, vmem],
        out_specs=hbm,
        scratch_shapes=[
            pltpu.VMEM((parts, m // parts, w), bf16),
            pltpu.SemaphoreType.DMA((parts,)),
        ],
        cost_estimate=cost(2 * i * m * w, 4 * (i + m) * w),
        compiler_params=params,
    )(coef, img)


def fold_kernel(n, *refs):
    parts, outs = refs[:n], refs[n:]
    at = 0
    for out in outs:
        rows = slice(at, at + out.shape[0])
        total = parts[0][rows]
        for part in parts[1:]:
            total = total + part[rows].astype(f32)
        out[...] = total.astype(out.dtype)
        at += out.shape[0]


def fold(size, *parts):
    n, w = parts[0].shape
    return pl.pallas_call(
        functools.partial(fold_kernel, len(parts)),
        out_shape=[
            jax.ShapeDtypeStruct((size, w), f32 if k == 0 else bf16) for k in range(n // size)
        ],
        in_specs=[vmem] * len(parts),
        out_specs=[vmem] * (n // size),
        cost_estimate=cost(n * w, 10 * n * w),
        compiler_params=params,
    )(*parts)


def backprop_kernel(unit, inv, proj, *refs):
    *parts, out, unit_buf, proj_buf, sems = refs
    reads = [
        pltpu.make_async_copy(unit, unit_buf, sems.at[0]),
        pltpu.make_async_copy(proj, proj_buf, sems.at[1]),
    ]
    for read in reads:
        read.start()
    total = 0.0
    for part in parts:
        if len(part.shape) == 2:
            total = total + part[...].astype(f32)
        else:
            for k in range(part.shape[0]):
                total = total + part[k].astype(f32)
    reads[0].wait()
    rows = unit_buf[...]
    along = jnp.sum(rows * total, axis=1, keepdims=True)
    delta = (inv[:, :1] * (total - rows * along)).astype(bf16)
    reads[1].wait()
    out[...] = lax.dot_general(
        delta, proj_buf[...], (((1,), (1,)), ((), ())), preferred_element_type=f32
    )


def backprop(unit, inv, proj, *parts):
    depth, width = proj.shape
    own = unit.shape[0]
    return pl.pallas_call(
        backprop_kernel,
        out_shape=jax.ShapeDtypeStruct((own, depth), f32),
        in_specs=[hbm, vmem, hbm] + [vmem] * len(parts),
        out_specs=vmem,
        scratch_shapes=[
            pltpu.VMEM(unit.shape, f32),
            pltpu.VMEM(proj.shape, bf16),
            pltpu.SemaphoreType.DMA((2,)),
        ],
        cost_estimate=cost(2 * own * depth * width, 2 * depth * width),
        compiler_params=params,
    )(far_off(unit), inv, far_off(proj), *parts)


def shards(image_feats, text_feats, image_proj, text_proj, log_temp, logit_bias):
    own = text_feats.shape[0]
    total = own * lax.axis_size(("y", "x", "core", "z"))
    send = lambda rows, axis, by: lax.ppermute(rows, axis, shift(axis, by))

    txt_unit, txt_inv, txt_rows = embed(text_feats, text_proj, lax.axis_size(("y", "x")))
    img_unit, img_inv, img_rows = embed(image_feats, image_proj, 1)
    txt_rows, img_rows = lax.optimization_barrier((txt_rows, img_rows))
    txt_rows = exchanged(txt_rows, ("y", "x")).reshape(-1, txt_rows.shape[2])
    img_rows = lax.all_gather(img_rows[0], "z", tiled=True)
    img_rows = lax.all_gather(img_rows, "core", tiled=True)

    coef, near, far = image_terms(
        own, log_temp, logit_bias, loss_scale / total, img_rows, txt_rows
    )
    far = send(far, "core", 1)
    txt_terms = text_terms(coef, img_rows)
    txt_terms = exchanged(txt_terms.reshape(-1, own, txt_terms.shape[1]), ("y", "x"))
    near, by1, by2, back = fold(3 * own, near, far)
    near, by4, by8 = fold(
        own, near, send(by1, "z", 1), send(by2, "z", 2), send(back, "z", -1)
    )
    image_grad = backprop(
        img_unit, img_inv, image_proj, near, send(by4, "z", 4), send(by8, "z", 8)
    )
    text_grad = backprop(txt_unit, txt_inv, text_proj, txt_terms)
    return (image_grad, text_grad)


def solution(mesh):
    blk, grp = mesh.devices.shape
    fine = Mesh(np.asarray(mesh.devices).reshape(blk // 8, 4, 2, grp), ("y", "x", "core", "z"))
    rows = P(("y", "x", "core", "z"), None)
    return jax.shard_map(
        shards,
        mesh=fine,
        in_specs=(rows, rows, P(), P(), P(), P()),
        out_specs=(rows, rows),
        check_vma=False,
    )
```

```python
import functools

import jax
import jax.numpy as jnp
import numpy as np
from jax import lax
from jax.experimental import pallas as pl
from jax.experimental.pallas import tpu as pltpu
from jax.sharding import Mesh
from jax.sharding import PartitionSpec as P

loss_scale = 65536.0
eps = 1e-06
f32 = jnp.float32
bf16 = jnp.bfloat16

vmem = pl.BlockSpec(memory_space=pltpu.VMEM)
smem = pl.BlockSpec(memory_space=pltpu.SMEM)
hbm = pl.BlockSpec(memory_space=pltpu.HBM)
params = pltpu.CompilerParams(vmem_limit_bytes=24 * 2**20)


def far_off(x):
    return pltpu.with_memory_space_constraint(x, pltpu.HBM)

ahead = (0, 4, 8, 1, 5, 9, 2, 6, 10, 11, 3, 7)


def cost(flops, moved, transcendentals=0):
    return pl.CostEstimate(flops=flops, bytes_accessed=moved, transcendentals=transcendentals)


def shift(axis, by):
    n = lax.axis_size(axis)
    return [(i, (i + by) % n) for i in range(n)]


def exchanged(copies, axis):
    return lax.all_to_all(copies, axis, 0, 0, tiled=True)


def embed_kernel(txt, txt_proj, img, img_proj, *refs):
    txt_unit, txt_inv, txt_rows, img_unit, img_inv, img_rows = refs[:6]
    txt_buf, txt_w, img_buf, img_w, unit_buf, rows_buf, sems, out_sems = refs[6:]
    cut = txt_w.shape[1]
    copies = txt_rows.shape[0]
    reads = []
    for feats, buf, proj, weights in ((txt, txt_buf, txt_proj, txt_w), (img, img_buf, img_proj, img_w)):
        reads.append([pltpu.make_async_copy(feats, buf, sems.at[sum(map(len, reads))])])
        for k in range(weights.shape[0]):
            reads[-1].append(
                pltpu.make_async_copy(
                    proj.at[pl.ds(k * cut, cut)], weights.at[k], sems.at[sum(map(len, reads))]
                )
            )
    for read in reads[0] + reads[1]:
        read.start()

    def unit_rows(buf, weights, arrivals):
        arrivals[0].wait()
        emb = jnp.zeros(unit_buf.shape[1:], f32)
        for k, arrival in enumerate(arrivals[1:]):
            arrival.wait()
            emb += jnp.dot(
                buf[:, k * cut : (k + 1) * cut], weights[k], preferred_element_type=f32
            )
        inv = lax.rsqrt(jnp.sum(emb * emb, axis=1, keepdims=True) + eps)
        return emb * inv, inv

    unit, inv = unit_rows(txt_buf, txt_w, reads[0])
    rows_buf[...] = unit.astype(bf16)
    writes = [
        pltpu.make_async_copy(rows_buf, txt_rows.at[k], out_sems.at[k]) for k in range(copies)
    ]
    for write in writes:
        write.start()
    unit_buf[0] = unit
    writes.append(pltpu.make_async_copy(unit_buf.at[0], txt_unit, out_sems.at[copies]))
    writes[-1].start()
    txt_inv[...] = jnp.broadcast_to(inv, txt_inv.shape)
    unit, inv = unit_rows(img_buf, img_w, reads[1])
    img_rows[...] = unit.astype(bf16)
    unit_buf[1] = unit
    writes.append(pltpu.make_async_copy(unit_buf.at[1], img_unit, out_sems.at[copies + 1]))
    writes[-1].start()
    img_inv[...] = jnp.broadcast_to(inv, img_inv.shape)
    for write in writes:
        write.wait()


def embed(txt, txt_proj, img, img_proj, copies):
    own, width = txt.shape[0], txt_proj.shape[1]
    cut = 512
    txt_cuts, img_cuts = txt.shape[1] // cut, img.shape[1] // cut
    unit, inv = pltpu.HBM((own, width), f32), jax.ShapeDtypeStruct((own, 128), f32)
    return pl.pallas_call(
        embed_kernel,
        out_shape=[
            unit,
            inv,
            pltpu.HBM((copies, own, width), bf16),
            unit,
            inv,
            jax.ShapeDtypeStruct((own, width), bf16),
        ],
        in_specs=[hbm] * 4,
        out_specs=[hbm, vmem, hbm, hbm, vmem, vmem],
        scratch_shapes=[
            pltpu.VMEM(txt.shape, bf16),
            pltpu.VMEM((txt_cuts, cut, width), bf16),
            pltpu.VMEM(img.shape, bf16),
            pltpu.VMEM((img_cuts, cut, width), bf16),
            pltpu.VMEM((2, own, width), f32),
            pltpu.VMEM((own, width), bf16),
            pltpu.SemaphoreType.DMA((txt_cuts + img_cuts + 2,)),
            pltpu.SemaphoreType.DMA((copies + 2,)),
        ],
        cost_estimate=cost(2 * own * width * (txt.shape[1] + img.shape[1]), 6 * 2**20),
        compiler_params=params,
    )(*map(far_off, (txt, txt_proj, img, img_proj)))


def image_kernel(own, factor, log_temp, bias, img, txt, coef_out, near_out, far_out, terms):
    nz = len(ahead)
    core = lax.axis_index("core")
    z = lax.axis_index("z")
    first_img = (core * nz + z) * own
    first_txt = lax.axis_index(("y", "x")) * own
    temp = jnp.exp(jnp.full((1, img.shape[0]), log_temp[0], f32))
    factor = factor * temp
    rows = img[...]
    size = 256
    total = 0.0
    for at in range(0, txt.shape[0], size):
        part = slice(at, at + size)
        logits = (
            lax.dot_general(
                txt[part], rows, (((1,), (1,)), ((), ())), preferred_element_type=f32
            )
            * temp
            + bias[0]
        )
        txt_ids = lax.broadcasted_iota(jnp.int32, logits.shape, 0) + (at - first_txt)
        img_ids = lax.broadcasted_iota(jnp.int32, logits.shape, 1) - first_img
        diag = ((txt_ids == img_ids) & (img_ids >= 0) & (img_ids < own)).astype(f32)
        coef = (factor * (jax.nn.sigmoid(logits) - diag)).astype(bf16)
        coef_out[part] = coef
        total = total + lax.dot_general(
            coef, txt[part], (((0,), (0,)), ((), ())), preferred_element_type=f32
        )
    terms[...] = total
    half = nz * own
    for k, by in enumerate(ahead):
        owner = lax.rem(z + by, nz) * own
        near = pl.multiple_of(core * half + owner, own)
        far = pl.multiple_of((1 - core) * half + owner, own)
        near_out[pl.ds(k * own, own)] = terms[pl.ds(near, own)]
        far_out[pl.ds(k * own, own)] = terms[pl.ds(far, own)].astype(bf16)


def image_terms(own, log_temp, bias, factor, img, txt):
    m, w = txt.shape
    i = img.shape[0]
    return pl.pallas_call(
        functools.partial(image_kernel, own, factor),
        out_shape=[
            jax.ShapeDtypeStruct((m, i), bf16),
            jax.ShapeDtypeStruct((i // 2, w), f32),
            jax.ShapeDtypeStruct((i // 2, w), bf16),
        ],
        in_specs=[smem, smem, vmem, vmem],
        out_specs=[vmem, vmem, vmem],
        scratch_shapes=[pltpu.VMEM((i, w), f32)],
        cost_estimate=cost(4 * i * m * w, 4 * (i + m) * w, i * m),
        compiler_params=params,
    )(log_temp, bias, img, txt)


def text_kernel(coef, img, out, buf, sems):
    rows = img[...]
    parts, size = buf.shape[:2]
    writes = []
    for q in range(parts):
        buf[q] = jnp.dot(
            coef[q * size : (q + 1) * size], rows, preferred_element_type=f32
        ).astype(bf16)
        writes.append(pltpu.make_async_copy(buf.at[q], out.at[pl.ds(q * size, size)], sems.at[q]))
        writes[-1].start()
    for write in writes:
        write.wait()


def text_terms(coef, img):
    m, i = coef.shape
    w = img.shape[1]
    parts = 2
    return pl.pallas_call(
        text_kernel,
        out_shape=pltpu.HBM((m, w), bf16),
        in_specs=[vmem, vmem],
        out_specs=hbm,
        scratch_shapes=[
            pltpu.VMEM((parts, m // parts, w), bf16),
            pltpu.SemaphoreType.DMA((parts,)),
        ],
        cost_estimate=cost(2 * i * m * w, 4 * (i + m) * w),
        compiler_params=params,
    )(coef, img)


def fold_kernel(n, *refs):
    parts, outs = refs[:n], refs[n:]
    at = 0
    for out in outs:
        rows = slice(at, at + out.shape[0])
        total = parts[0][rows]
        for part in parts[1:]:
            total = total + part[rows].astype(f32)
        out[...] = total.astype(out.dtype)
        at += out.shape[0]


def fold(size, *parts):
    n, w = parts[0].shape
    work = 10**10
    return pl.pallas_call(
        functools.partial(fold_kernel, len(parts)),
        out_shape=[
            jax.ShapeDtypeStruct((size, w), f32 if k == 0 else bf16) for k in range(n // size)
        ],
        in_specs=[vmem] * len(parts),
        out_specs=[vmem] * (n // size),
        cost_estimate=cost(work, 10 * n * w),
        compiler_params=params,
    )(*parts)


def backprop_kernel(unit, inv, proj, *refs):
    *parts, out, unit_buf, proj_buf, sems = refs
    cuts, cut = proj_buf.shape[:2]
    reads = [pltpu.make_async_copy(unit, unit_buf, sems.at[cuts])]
    for k in range(cuts):
        reads.append(pltpu.make_async_copy(proj.at[pl.ds(k * cut, cut)], proj_buf.at[k], sems.at[k]))
    for read in reads:
        read.start()
    total = 0.0
    for part in parts:
        if len(part.shape) == 2:
            total = total + part[...].astype(f32)
        else:
            for k in range(part.shape[0]):
                total = total + part[k].astype(f32)
    reads[0].wait()
    rows = unit_buf[...]
    along = jnp.sum(rows * total, axis=1, keepdims=True)
    delta = (inv[:, :1] * (total - rows * along)).astype(bf16)
    for k in range(cuts):
        reads[k + 1].wait()
        out[:, k * cut : (k + 1) * cut] = lax.dot_general(
            delta, proj_buf[k], (((1,), (1,)), ((), ())), preferred_element_type=f32
        )


def backprop(unit, inv, proj, *parts):
    depth, width = proj.shape
    own = unit.shape[0]
    cut = 512
    return pl.pallas_call(
        backprop_kernel,
        out_shape=jax.ShapeDtypeStruct((own, depth), f32),
        in_specs=[hbm, vmem, hbm] + [vmem] * len(parts),
        out_specs=vmem,
        scratch_shapes=[
            pltpu.VMEM(unit.shape, f32),
            pltpu.VMEM((depth // cut, cut, width), bf16),
            pltpu.SemaphoreType.DMA((depth // cut + 1,)),
        ],
        cost_estimate=cost(2 * own * depth * width, 2 * depth * width),
        compiler_params=params,
    )(far_off(unit), inv, far_off(proj), *parts)


def shards(image_feats, text_feats, image_proj, text_proj, log_temp, logit_bias):
    own = text_feats.shape[0]
    total = own * lax.axis_size(("y", "x", "core", "z"))
    send = lambda rows, axis, by: lax.ppermute(rows, axis, shift(axis, by))

    copies = lax.axis_size(("y", "x"))
    txt_unit, txt_inv, txt_rows, img_unit, img_inv, img_rows = embed(
        text_feats, text_proj, image_feats, image_proj, copies
    )
    txt_rows = exchanged(txt_rows, ("y", "x")).reshape(-1, txt_rows.shape[2])
    img_rows = lax.all_gather(img_rows, "z", tiled=True)
    img_rows = lax.all_gather(img_rows, "core", tiled=True)

    coef, near, far = image_terms(
        own, log_temp, logit_bias, loss_scale / total, img_rows, txt_rows
    )
    far = send(far, "core", 1)
    txt_terms = text_terms(coef, img_rows)
    txt_terms = exchanged(txt_terms.reshape(-1, own, txt_terms.shape[1]), ("y", "x"))
    near, by1, by2, back = fold(3 * own, near, far)
    near, by4, by8 = fold(
        own, near, send(by1, "z", 1), send(by2, "z", 2), send(back, "z", -1)
    )
    text_grad = backprop(txt_unit, txt_inv, text_proj, txt_terms)
    got = (send(by4, "z", 4), send(by8, "z", 8))
    near, text_grad = lax.optimization_barrier((near, text_grad))
    image_grad = backprop(img_unit, img_inv, image_proj, near, *got)
    return (image_grad, text_grad)


def solution(mesh):
    blk, grp = mesh.devices.shape
    fine = Mesh(np.asarray(mesh.devices).reshape(blk // 8, 4, 2, grp), ("y", "x", "core", "z"))
    rows = P(("y", "x", "core", "z"), None)
    return jax.shard_map(
        shards,
        mesh=fine,
        in_specs=(rows, rows, P(), P(), P(), P()),
        out_specs=(rows, rows),
        check_vma=False,
    )
```

```python
import functools

import jax
import jax.numpy as jnp
import numpy as np
from jax import lax
from jax.experimental import pallas as pl
from jax.experimental.pallas import tpu as pltpu
from jax.sharding import Mesh
from jax.sharding import PartitionSpec as P

loss_scale = 65536.0
eps = 1e-06
f32 = jnp.float32
bf16 = jnp.bfloat16

vmem = pl.BlockSpec(memory_space=pltpu.VMEM)
smem = pl.BlockSpec(memory_space=pltpu.SMEM)
hbm = pl.BlockSpec(memory_space=pltpu.HBM)
params = pltpu.CompilerParams(vmem_limit_bytes=24 * 2**20)


def far_off(x):
    return pltpu.with_memory_space_constraint(x, pltpu.HBM)

ahead = (0, 4, 8, 1, 5, 9, 2, 6, 10, 11, 3, 7)


def cost(flops, moved, transcendentals=0):
    return pl.CostEstimate(flops=flops, bytes_accessed=moved, transcendentals=transcendentals)


def shift(axis, by):
    n = lax.axis_size(axis)
    return [(i, (i + by) % n) for i in range(n)]


def exchanged(copies, axis):
    return lax.all_to_all(copies, axis, 0, 0, tiled=True)


def repeat_kernel(rows, out, buf, sems):
    read = pltpu.make_async_copy(rows, buf, sems.at[0])
    read.start()
    read.wait()
    writes = [pltpu.make_async_copy(buf, out.at[k], sems.at[k + 1]) for k in range(out.shape[0])]
    for write in writes:
        write.start()
    for write in writes:
        write.wait()


def repeated(rows, n):
    return pl.pallas_call(
        repeat_kernel,
        out_shape=pltpu.HBM((n,) + rows.shape, rows.dtype),
        in_specs=[hbm],
        out_specs=hbm,
        scratch_shapes=[pltpu.VMEM(rows.shape, rows.dtype), pltpu.SemaphoreType.DMA((n + 1,))],
        cost_estimate=cost(0, 2 * n * rows.size),
        compiler_params=params,
    )(far_off(rows))


def normed(emb):
    inv = lax.rsqrt(jnp.sum(emb * emb, axis=1, keepdims=True) + eps)
    return emb * inv, inv


def embed_kernel(feats, proj, unit_out, inv_out, rows_out, buf, weights, unit_buf, sems):
    cuts, cut = weights.shape[:2]
    reads = [pltpu.make_async_copy(feats, buf, sems.at[cuts])]
    for k in range(cuts):
        reads.append(pltpu.make_async_copy(proj.at[pl.ds(k * cut, cut)], weights.at[k], sems.at[k]))
    for read in reads:
        read.start()
    reads[0].wait()
    emb = jnp.zeros(rows_out.shape, f32)
    for k in range(cuts):
        reads[k + 1].wait()
        emb += jnp.dot(buf[:, k * cut : (k + 1) * cut], weights[k], preferred_element_type=f32)
    unit, inv = normed(emb)
    unit_buf[...] = unit
    write = pltpu.make_async_copy(unit_buf, unit_out, sems.at[cuts + 1])
    write.start()
    rows_out[...] = unit.astype(bf16)
    inv_out[...] = jnp.broadcast_to(inv, inv_out.shape)
    write.wait()


def embed(feats, proj):
    own, depth = feats.shape
    width = proj.shape[1]
    cut = 512
    return pl.pallas_call(
        embed_kernel,
        out_shape=[
            pltpu.HBM((own, width), f32),
            jax.ShapeDtypeStruct((own, 128), f32),
            jax.ShapeDtypeStruct((own, width), bf16),
        ],
        in_specs=[hbm, hbm],
        out_specs=[hbm, vmem, vmem],
        scratch_shapes=[
            pltpu.VMEM(feats.shape, bf16),
            pltpu.VMEM((depth // cut, cut, width), bf16),
            pltpu.VMEM((own, width), f32),
            pltpu.SemaphoreType.DMA((depth // cut + 2,)),
        ],
        cost_estimate=cost(2 * own * depth * width, 2 * depth * width),
        compiler_params=params,
    )(far_off(feats), far_off(proj))


def tile_kernel(own, factor, log_temp, bias, img, feats, proj, *refs):
    unit_out, inv_out, coef_out, near_out, far_out, units, invs, terms, sem = refs
    nz = len(ahead)
    core = lax.axis_index("core")
    z = lax.axis_index("z")
    first_img = (core * nz + z) * own
    first_txt = lax.axis_index(("y", "x")) * own
    temp = jnp.exp(jnp.full((1, img.shape[0]), log_temp[0], f32))
    factor = factor * temp
    rows = img[...]
    weights = proj[...]
    size = min(256, feats.shape[0])
    total = 0.0
    for at in range(0, feats.shape[0], size):
        part = slice(at, at + size)
        unit, inv = normed(jnp.dot(feats[part], weights, preferred_element_type=f32))
        units[part] = unit
        invs[part] = jnp.broadcast_to(inv, (size, 128))
        txt = unit.astype(bf16)
        logits = (
            lax.dot_general(txt, rows, (((1,), (1,)), ((), ())), preferred_element_type=f32) * temp
            + bias[0]
        )
        txt_ids = lax.broadcasted_iota(jnp.int32, logits.shape, 0) + (at - first_txt)
        img_ids = lax.broadcasted_iota(jnp.int32, logits.shape, 1) - first_img
        diag = ((txt_ids == img_ids) & (img_ids >= 0) & (img_ids < own)).astype(f32)
        coef = (factor * (jax.nn.sigmoid(logits) - diag)).astype(bf16)
        coef_out[part] = coef
        total = total + lax.dot_general(
            coef, txt, (((0,), (0,)), ((), ())), preferred_element_type=f32
        )
    mine = pl.ds(pl.multiple_of(first_txt, own), own)
    write = pltpu.make_async_copy(units.at[mine], unit_out, sem)
    write.start()
    inv_out[...] = invs[mine]
    terms[...] = total
    half = nz * own
    for k, by in enumerate(ahead):
        owner = lax.rem(z + by, nz) * own
        near = pl.multiple_of(core * half + owner, own)
        far = pl.multiple_of((1 - core) * half + owner, own)
        near_out[pl.ds(k * own, own)] = terms[pl.ds(near, own)]
        far_out[pl.ds(k * own, own)] = terms[pl.ds(far, own)].astype(bf16)
    write.wait()


def tile(own, log_temp, bias, factor, img, feats, proj):
    m = feats.shape[0]
    i, w = img.shape
    return pl.pallas_call(
        functools.partial(tile_kernel, own, factor),
        out_shape=[
            pltpu.HBM((own, w), f32),
            jax.ShapeDtypeStruct((own, 128), f32),
            jax.ShapeDtypeStruct((m, i), bf16),
            jax.ShapeDtypeStruct((i // 2, w), f32),
            jax.ShapeDtypeStruct((i // 2, w), bf16),
        ],
        in_specs=[smem, smem, vmem, vmem, vmem],
        out_specs=[hbm, vmem, vmem, vmem, vmem],
        scratch_shapes=[
            pltpu.VMEM((m, w), f32),
            pltpu.VMEM((m, 128), f32),
            pltpu.VMEM((i, w), f32),
            pltpu.SemaphoreType.DMA,
        ],
        cost_estimate=cost(4 * i * m * w + 2 * feats.size * w, 4 * (i + m) * w, i * m),
        compiler_params=params,
    )(log_temp, bias, img, feats, proj)


def text_kernel(coef, img, out, buf, sems):
    rows = img[...]
    parts, size = buf.shape[:2]
    writes = []
    for q in range(parts):
        buf[q] = jnp.dot(
            coef[q * size : (q + 1) * size], rows, preferred_element_type=f32
        ).astype(bf16)
        writes.append(pltpu.make_async_copy(buf.at[q], out.at[pl.ds(q * size, size)], sems.at[q]))
        writes[-1].start()
    for write in writes:
        write.wait()


def text_terms(coef, img):
    m, i = coef.shape
    w = img.shape[1]
    parts = 2
    return pl.pallas_call(
        text_kernel,
        out_shape=pltpu.HBM((m, w), bf16),
        in_specs=[vmem, vmem],
        out_specs=hbm,
        scratch_shapes=[
            pltpu.VMEM((parts, m // parts, w), bf16),
            pltpu.SemaphoreType.DMA((parts,)),
        ],
        cost_estimate=cost(2 * i * m * w, 4 * (i + m) * w),
        compiler_params=params,
    )(coef, img)


def fold_kernel(n, *refs):
    parts, outs = refs[:n], refs[n:]
    at = 0
    for out in outs:
        rows = slice(at, at + out.shape[0])
        total = parts[0][rows]
        for part in parts[1:]:
            total = total + part[rows].astype(f32)
        out[...] = total.astype(out.dtype)
        at += out.shape[0]


def fold(size, *parts):
    n, w = parts[0].shape
    work = 10**10
    return pl.pallas_call(
        functools.partial(fold_kernel, len(parts)),
        out_shape=[
            jax.ShapeDtypeStruct((size, w), f32 if k == 0 else bf16) for k in range(n // size)
        ],
        in_specs=[vmem] * len(parts),
        out_specs=[vmem] * (n // size),
        cost_estimate=cost(work, 10 * n * w),
        compiler_params=params,
    )(*parts)


def backprop_kernel(unit, inv, proj, *refs):
    *parts, out, unit_buf, proj_buf, sems = refs
    cuts, cut = proj_buf.shape[:2]
    reads = [pltpu.make_async_copy(unit, unit_buf, sems.at[cuts])]
    for k in range(cuts):
        reads.append(pltpu.make_async_copy(proj.at[pl.ds(k * cut, cut)], proj_buf.at[k], sems.at[k]))
    for read in reads:
        read.start()
    total = 0.0
    for part in parts:
        if len(part.shape) == 2:
            total = total + part[...].astype(f32)
        else:
            for k in range(part.shape[0]):
                total = total + part[k].astype(f32)
    reads[0].wait()
    rows = unit_buf[...]
    along = jnp.sum(rows * total, axis=1, keepdims=True)
    delta = (inv[:, :1] * (total - rows * along)).astype(bf16)
    for k in range(cuts):
        reads[k + 1].wait()
        out[:, k * cut : (k + 1) * cut] = lax.dot_general(
            delta, proj_buf[k], (((1,), (1,)), ((), ())), preferred_element_type=f32
        )


def backprop(unit, inv, proj, *parts):
    depth, width = proj.shape
    own = unit.shape[0]
    cut = 512
    return pl.pallas_call(
        backprop_kernel,
        out_shape=jax.ShapeDtypeStruct((own, depth), f32),
        in_specs=[hbm, vmem, hbm] + [vmem] * len(parts),
        out_specs=vmem,
        scratch_shapes=[
            pltpu.VMEM(unit.shape, f32),
            pltpu.VMEM((depth // cut, cut, width), bf16),
            pltpu.SemaphoreType.DMA((depth // cut + 1,)),
        ],
        cost_estimate=cost(2 * own * depth * width, 2 * depth * width),
        compiler_params=params,
    )(far_off(unit), inv, far_off(proj), *parts)


def shards(image_feats, text_feats, image_proj, text_proj, log_temp, logit_bias):
    own = text_feats.shape[0]
    total = own * lax.axis_size(("y", "x", "core", "z"))
    send = lambda rows, axis, by: lax.ppermute(rows, axis, shift(axis, by))

    plane = ("y", "x")
    feats = exchanged(repeated(text_feats, lax.axis_size(plane)), plane)
    feats = feats.reshape(-1, text_feats.shape[1])
    img_unit, img_inv, img_rows = embed(image_feats, image_proj)
    img_rows = lax.all_gather(img_rows, "z", tiled=True)
    img_rows = lax.all_gather(img_rows, "core", tiled=True)

    txt_unit, txt_inv, coef, near, far = tile(
        own, log_temp, logit_bias, loss_scale / total, img_rows, feats, text_proj
    )
    far = send(far, "core", 1)
    txt_terms = text_terms(coef, img_rows)
    txt_terms = exchanged(txt_terms.reshape(-1, own, txt_terms.shape[1]), plane)
    near, by1, by2, back = fold(3 * own, near, far)
    near, by4, by8 = fold(
        own, near, send(by1, "z", 1), send(by2, "z", 2), send(back, "z", -1)
    )
    image_grad = backprop(
        img_unit, img_inv, image_proj, near, send(by4, "z", 4), send(by8, "z", 8)
    )
    text_grad = backprop(txt_unit, txt_inv, text_proj, txt_terms)
    return (image_grad, text_grad)


def solution(mesh):
    blk, grp = mesh.devices.shape
    fine = Mesh(np.asarray(mesh.devices).reshape(blk // 8, 4, 2, grp), ("y", "x", "core", "z"))
    rows = P(("y", "x", "core", "z"), None)
    return jax.shard_map(
        shards,
        mesh=fine,
        in_specs=(rows, rows, P(), P(), P(), P()),
        out_specs=(rows, rows),
        check_vma=False,
    )
```

```python
import functools

import jax
import jax.numpy as jnp
import numpy as np
from jax import lax
from jax.experimental import pallas as pl
from jax.experimental.pallas import tpu as pltpu
from jax.sharding import Mesh
from jax.sharding import PartitionSpec as P

loss_scale = 65536.0
eps = 1e-06
f32 = jnp.float32
bf16 = jnp.bfloat16

vmem = pl.BlockSpec(memory_space=pltpu.VMEM)
smem = pl.BlockSpec(memory_space=pltpu.SMEM)
hbm = pl.BlockSpec(memory_space=pltpu.HBM)
params = pltpu.CompilerParams(vmem_limit_bytes=24 * 2**20)


def far_off(x):
    return pltpu.with_memory_space_constraint(x, pltpu.HBM)

ahead = (0, 4, 8, 1, 5, 9, 2, 6, 10, 11, 3, 7)


def cost(flops, moved, transcendentals=0):
    return pl.CostEstimate(flops=flops, bytes_accessed=moved, transcendentals=transcendentals)


def shift(axis, by):
    n = lax.axis_size(axis)
    return [(i, (i + by) % n) for i in range(n)]


def exchanged(copies, axis):
    return lax.all_to_all(copies, axis, 0, 0, tiled=True)


def embed_kernel(txt, txt_proj, img, img_proj, *refs):
    txt_unit, txt_inv, txt_rows, img_unit, img_inv, img_rows = refs[:6]
    txt_buf, txt_w, img_buf, img_w, unit_buf, rows_buf, sems, out_sems = refs[6:]
    cut = txt_w.shape[1]
    copies = txt_rows.shape[0]
    reads = []
    for feats, buf, proj, weights in ((txt, txt_buf, txt_proj, txt_w), (img, img_buf, img_proj, img_w)):
        reads.append([pltpu.make_async_copy(feats, buf, sems.at[sum(map(len, reads))])])
        for k in range(weights.shape[0]):
            reads[-1].append(
                pltpu.make_async_copy(
                    proj.at[pl.ds(k * cut, cut)], weights.at[k], sems.at[sum(map(len, reads))]
                )
            )
    for read in reads[0] + reads[1]:
        read.start()

    def unit_rows(buf, weights, arrivals):
        arrivals[0].wait()
        emb = jnp.zeros(unit_buf.shape[1:], f32)
        for k, arrival in enumerate(arrivals[1:]):
            arrival.wait()
            emb += jnp.dot(
                buf[:, k * cut : (k + 1) * cut], weights[k], preferred_element_type=f32
            )
        inv = lax.rsqrt(jnp.sum(emb * emb, axis=1, keepdims=True) + eps)
        return emb * inv, inv

    unit, inv = unit_rows(txt_buf, txt_w, reads[0])
    rows_buf[...] = unit.astype(bf16)
    writes = [
        pltpu.make_async_copy(rows_buf, txt_rows.at[k], out_sems.at[k]) for k in range(copies)
    ]
    for write in writes:
        write.start()
    unit_buf[0] = unit
    writes.append(pltpu.make_async_copy(unit_buf.at[0], txt_unit, out_sems.at[copies]))
    writes[-1].start()
    txt_inv[...] = jnp.broadcast_to(inv, txt_inv.shape)
    unit, inv = unit_rows(img_buf, img_w, reads[1])
    img_rows[...] = unit.astype(bf16)
    unit_buf[1] = unit
    writes.append(pltpu.make_async_copy(unit_buf.at[1], img_unit, out_sems.at[copies + 1]))
    writes[-1].start()
    img_inv[...] = jnp.broadcast_to(inv, img_inv.shape)
    for write in writes:
        write.wait()


def embed(txt, txt_proj, img, img_proj, copies):
    own, width = txt.shape[0], txt_proj.shape[1]
    cut = 512
    txt_cuts, img_cuts = txt.shape[1] // cut, img.shape[1] // cut
    unit, inv = pltpu.HBM((own, width), f32), jax.ShapeDtypeStruct((own, 128), f32)
    return pl.pallas_call(
        embed_kernel,
        out_shape=[
            unit,
            inv,
            pltpu.HBM((copies, own, width), bf16),
            unit,
            inv,
            jax.ShapeDtypeStruct((own, width), bf16),
        ],
        in_specs=[hbm] * 4,
        out_specs=[hbm, vmem, hbm, hbm, vmem, vmem],
        scratch_shapes=[
            pltpu.VMEM(txt.shape, bf16),
            pltpu.VMEM((txt_cuts, cut, width), bf16),
            pltpu.VMEM(img.shape, bf16),
            pltpu.VMEM((img_cuts, cut, width), bf16),
            pltpu.VMEM((2, own, width), f32),
            pltpu.VMEM((own, width), bf16),
            pltpu.SemaphoreType.DMA((txt_cuts + img_cuts + 2,)),
            pltpu.SemaphoreType.DMA((copies + 2,)),
        ],
        cost_estimate=cost(2 * own * width * (txt.shape[1] + img.shape[1]), 6 * 2**20),
        compiler_params=params,
    )(*map(far_off, (txt, txt_proj, img, img_proj)))


def image_kernel(own, factor, log_temp, bias, img, txt, coef_out, near_out, far_out, terms):
    nz = len(ahead)
    core = lax.axis_index("core")
    z = lax.axis_index("z")
    first_img = (core * nz + z) * own
    first_txt = lax.axis_index(("y", "x")) * own
    temp = jnp.exp(jnp.full((1, img.shape[0]), log_temp[0], f32))
    factor = factor * temp
    rows = img[...]
    size = 256
    total = 0.0
    for at in range(0, txt.shape[0], size):
        part = slice(at, at + size)
        logits = (
            lax.dot_general(
                txt[part], rows, (((1,), (1,)), ((), ())), preferred_element_type=f32
            )
            * temp
            + bias[0]
        )
        txt_ids = lax.broadcasted_iota(jnp.int32, logits.shape, 0) + (at - first_txt)
        img_ids = lax.broadcasted_iota(jnp.int32, logits.shape, 1) - first_img
        diag = ((txt_ids == img_ids) & (img_ids >= 0) & (img_ids < own)).astype(f32)
        coef = (factor * (jax.nn.sigmoid(logits) - diag)).astype(bf16)
        coef_out[part] = coef
        total = total + lax.dot_general(
            coef, txt[part], (((0,), (0,)), ((), ())), preferred_element_type=f32
        )
    terms[...] = total
    half = nz * own
    for k, by in enumerate(ahead):
        owner = lax.rem(z + by, nz) * own
        near = pl.multiple_of(core * half + owner, own)
        far = pl.multiple_of((1 - core) * half + owner, own)
        near_out[pl.ds(k * own, own)] = terms[pl.ds(near, own)]
        far_out[pl.ds(k * own, own)] = terms[pl.ds(far, own)].astype(bf16)


def image_terms(own, log_temp, bias, factor, img, txt):
    m, w = txt.shape
    i = img.shape[0]
    return pl.pallas_call(
        functools.partial(image_kernel, own, factor),
        out_shape=[
            jax.ShapeDtypeStruct((m, i), bf16),
            jax.ShapeDtypeStruct((i // 2, w), f32),
            jax.ShapeDtypeStruct((i // 2, w), bf16),
        ],
        in_specs=[smem, smem, vmem, vmem],
        out_specs=[vmem, vmem, vmem],
        scratch_shapes=[pltpu.VMEM((i, w), f32)],
        cost_estimate=cost(4 * i * m * w, 4 * (i + m) * w, i * m),
        compiler_params=params,
    )(log_temp, bias, img, txt)


def text_kernel(coef, img, out, buf, sems):
    rows = img[...]
    parts, size = buf.shape[:2]
    writes = []
    for q in range(parts):
        buf[q] = jnp.dot(
            coef[q * size : (q + 1) * size], rows, preferred_element_type=f32
        ).astype(bf16)
        writes.append(pltpu.make_async_copy(buf.at[q], out.at[pl.ds(q * size, size)], sems.at[q]))
        writes[-1].start()
    for write in writes:
        write.wait()


def text_terms(coef, img):
    m, i = coef.shape
    w = img.shape[1]
    parts = 2
    return pl.pallas_call(
        text_kernel,
        out_shape=pltpu.HBM((m, w), bf16),
        in_specs=[vmem, vmem],
        out_specs=hbm,
        scratch_shapes=[
            pltpu.VMEM((parts, m // parts, w), bf16),
            pltpu.SemaphoreType.DMA((parts,)),
        ],
        cost_estimate=cost(2 * i * m * w, 4 * (i + m) * w),
        compiler_params=params,
    )(coef, img)


def fold_kernel(n, *refs):
    parts, outs = refs[:n], refs[n:]
    at = 0
    for out in outs:
        rows = slice(at, at + out.shape[0])
        total = parts[0][rows]
        for part in parts[1:]:
            total = total + part[rows].astype(f32)
        out[...] = total.astype(out.dtype)
        at += out.shape[0]


def fold(size, *parts):
    n, w = parts[0].shape
    work = 10**10
    return pl.pallas_call(
        functools.partial(fold_kernel, len(parts)),
        out_shape=[
            jax.ShapeDtypeStruct((size, w), f32 if k == 0 else bf16) for k in range(n // size)
        ],
        in_specs=[vmem] * len(parts),
        out_specs=[vmem] * (n // size),
        cost_estimate=cost(work, 10 * n * w),
        compiler_params=params,
    )(*parts)


def backprop_kernel(unit, inv, proj, *refs):
    *parts, out, unit_buf, proj_buf, sems = refs
    cuts, cut = proj_buf.shape[:2]
    reads = [pltpu.make_async_copy(unit, unit_buf, sems.at[cuts])]
    for k in range(cuts):
        reads.append(pltpu.make_async_copy(proj.at[pl.ds(k * cut, cut)], proj_buf.at[k], sems.at[k]))
    for read in reads:
        read.start()
    total = 0.0
    for part in parts:
        if len(part.shape) == 2:
            total = total + part[...].astype(f32)
        else:
            for k in range(part.shape[0]):
                total = total + part[k].astype(f32)
    reads[0].wait()
    rows = unit_buf[...]
    along = jnp.sum(rows * total, axis=1, keepdims=True)
    delta = (inv[:, :1] * (total - rows * along)).astype(bf16)
    for k in range(cuts):
        reads[k + 1].wait()
        out[:, k * cut : (k + 1) * cut] = lax.dot_general(
            delta, proj_buf[k], (((1,), (1,)), ((), ())), preferred_element_type=f32
        )


def backprop(unit, inv, proj, *parts):
    depth, width = proj.shape
    own = unit.shape[0]
    cut = 512
    return pl.pallas_call(
        backprop_kernel,
        out_shape=jax.ShapeDtypeStruct((own, depth), f32),
        in_specs=[hbm, vmem, hbm] + [vmem] * len(parts),
        out_specs=vmem,
        scratch_shapes=[
            pltpu.VMEM(unit.shape, f32),
            pltpu.VMEM((depth // cut, cut, width), bf16),
            pltpu.SemaphoreType.DMA((depth // cut + 1,)),
        ],
        cost_estimate=cost(2 * own * depth * width, 2 * depth * width),
        compiler_params=params,
    )(far_off(unit), inv, far_off(proj), *parts)


def shards(image_feats, text_feats, image_proj, text_proj, log_temp, logit_bias):
    own = text_feats.shape[0]
    total = own * lax.axis_size(("y", "x", "core", "z"))
    send = lambda rows, axis, by: lax.ppermute(rows, axis, shift(axis, by))

    copies = lax.axis_size(("y", "x"))
    txt_unit, txt_inv, txt_rows, img_unit, img_inv, img_rows = embed(
        text_feats, text_proj, image_feats, image_proj, copies
    )
    txt_rows = exchanged(txt_rows, ("y", "x")).reshape(-1, txt_rows.shape[2])
    img_rows = lax.all_gather(img_rows, "z", tiled=True)
    img_rows = lax.all_gather(img_rows, "core", tiled=True)

    coef, near, far = image_terms(
        own, log_temp, logit_bias, loss_scale / total, img_rows, txt_rows
    )
    far = send(far, "core", 1)
    txt_terms = text_terms(coef, img_rows)
    txt_terms = exchanged(txt_terms.reshape(-1, own, txt_terms.shape[1]), ("y", "x"))
    near, by1, by2, back = fold(3 * own, near, far)
    near, by4, by8 = fold(
        own, near, send(by1, "z", 1), send(by2, "z", 2), send(back, "z", -1)
    )
    image_grad = backprop(
        img_unit, img_inv, image_proj, near, send(by4, "z", 4), send(by8, "z", 8)
    )
    text_grad = backprop(txt_unit, txt_inv, text_proj, txt_terms)
    return (image_grad, text_grad)


def solution(mesh):
    blk, grp = mesh.devices.shape
    fine = Mesh(np.asarray(mesh.devices).reshape(blk // 8, 4, 2, grp), ("y", "x", "core", "z"))
    rows = P(("y", "x", "core", "z"), None)
    return jax.shard_map(
        shards,
        mesh=fine,
        in_specs=(rows, rows, P(), P(), P(), P()),
        out_specs=(rows, rows),
        check_vma=False,
    )
```

```python
import functools

import jax
import jax.numpy as jnp
import numpy as np
from jax import lax
from jax.experimental import pallas as pl
from jax.experimental.pallas import tpu as pltpu
from jax.sharding import Mesh
from jax.sharding import PartitionSpec as P

loss_scale = 65536.0
eps = 1e-06
f32 = jnp.float32
bf16 = jnp.bfloat16

vmem = pl.BlockSpec(memory_space=pltpu.VMEM)
smem = pl.BlockSpec(memory_space=pltpu.SMEM)
hbm = pl.BlockSpec(memory_space=pltpu.HBM)
params = pltpu.CompilerParams(vmem_limit_bytes=24 * 2**20)


def far_off(x):
    return pltpu.with_memory_space_constraint(x, pltpu.HBM)

ahead = (0, 4, 8, 1, 5, 9, 2, 6, 10, 11, 3, 7)


def cost(flops, moved, transcendentals=0):
    return pl.CostEstimate(flops=flops, bytes_accessed=moved, transcendentals=transcendentals)


def shift(axis, by):
    n = lax.axis_size(axis)
    return [(i, (i + by) % n) for i in range(n)]


def exchanged(copies, axis):
    return lax.all_to_all(copies, axis, 0, 0, tiled=True)


def embed_kernel(txt, txt_proj, img, img_proj, *refs):
    txt_unit, txt_inv, txt_rows, img_unit, img_inv, img_rows = refs[:6]
    txt_buf, txt_w, img_buf, img_w, unit_buf, rows_buf, sems, out_sems = refs[6:]
    cut = txt_w.shape[1]
    copies = txt_rows.shape[0]
    reads = []
    for feats, buf, proj, weights in ((txt, txt_buf, txt_proj, txt_w), (img, img_buf, img_proj, img_w)):
        reads.append([pltpu.make_async_copy(feats, buf, sems.at[sum(map(len, reads))])])
        for k in range(weights.shape[0]):
            reads[-1].append(
                pltpu.make_async_copy(
                    proj.at[pl.ds(k * cut, cut)], weights.at[k], sems.at[sum(map(len, reads))]
                )
            )
    for read in reads[0] + reads[1]:
        read.start()

    def unit_rows(buf, weights, arrivals):
        arrivals[0].wait()
        emb = jnp.zeros(unit_buf.shape[1:], f32)
        for k, arrival in enumerate(arrivals[1:]):
            arrival.wait()
            emb += jnp.dot(
                buf[:, k * cut : (k + 1) * cut], weights[k], preferred_element_type=f32
            )
        inv = lax.rsqrt(jnp.sum(emb * emb, axis=1, keepdims=True) + eps)
        return emb * inv, inv

    unit, inv = unit_rows(txt_buf, txt_w, reads[0])
    rows_buf[...] = unit.astype(bf16)
    writes = [
        pltpu.make_async_copy(rows_buf, txt_rows.at[k], out_sems.at[k]) for k in range(copies)
    ]
    for write in writes:
        write.start()
    unit_buf[0] = unit
    writes.append(pltpu.make_async_copy(unit_buf.at[0], txt_unit, out_sems.at[copies]))
    writes[-1].start()
    txt_inv[...] = jnp.broadcast_to(inv, txt_inv.shape)
    unit, inv = unit_rows(img_buf, img_w, reads[1])
    img_rows[...] = unit.astype(bf16)
    unit_buf[1] = unit
    writes.append(pltpu.make_async_copy(unit_buf.at[1], img_unit, out_sems.at[copies + 1]))
    writes[-1].start()
    img_inv[...] = jnp.broadcast_to(inv, img_inv.shape)
    for write in writes:
        write.wait()


def embed(txt, txt_proj, img, img_proj, copies):
    own, width = txt.shape[0], txt_proj.shape[1]
    cut = 512
    txt_cuts, img_cuts = txt.shape[1] // cut, img.shape[1] // cut
    unit, inv = pltpu.HBM((own, width), f32), jax.ShapeDtypeStruct((own, 128), f32)
    return pl.pallas_call(
        embed_kernel,
        out_shape=[
            unit,
            inv,
            pltpu.HBM((copies, own, width), bf16),
            unit,
            inv,
            jax.ShapeDtypeStruct((own, width), bf16),
        ],
        in_specs=[hbm] * 4,
        out_specs=[hbm, vmem, hbm, hbm, vmem, vmem],
        scratch_shapes=[
            pltpu.VMEM(txt.shape, bf16),
            pltpu.VMEM((txt_cuts, cut, width), bf16),
            pltpu.VMEM(img.shape, bf16),
            pltpu.VMEM((img_cuts, cut, width), bf16),
            pltpu.VMEM((2, own, width), f32),
            pltpu.VMEM((own, width), bf16),
            pltpu.SemaphoreType.DMA((txt_cuts + img_cuts + 2,)),
            pltpu.SemaphoreType.DMA((copies + 2,)),
        ],
        cost_estimate=cost(2 * own * width * (txt.shape[1] + img.shape[1]), 6 * 2**20),
        compiler_params=params,
    )(*map(far_off, (txt, txt_proj, img, img_proj)))


def image_kernel(own, factor, log_temp, bias, img, txt, coef_out, near_out, far_out, terms):
    nz = len(ahead)
    core = lax.axis_index("core")
    z = lax.axis_index("z")
    first_img = (core * nz + z) * own
    first_txt = lax.axis_index(("y", "x")) * own
    temp = jnp.exp(jnp.full((1, img.shape[0]), log_temp[0], f32))
    factor = factor * temp
    rows = img[...]
    size = 256
    total = 0.0
    for at in range(0, txt.shape[0], size):
        part = slice(at, at + size)
        logits = (
            lax.dot_general(
                txt[part], rows, (((1,), (1,)), ((), ())), preferred_element_type=f32
            )
            * temp
            + bias[0]
        )
        txt_ids = lax.broadcasted_iota(jnp.int32, logits.shape, 0) + (at - first_txt)
        img_ids = lax.broadcasted_iota(jnp.int32, logits.shape, 1) - first_img
        diag = ((txt_ids == img_ids) & (img_ids >= 0) & (img_ids < own)).astype(f32)
        coef = (factor * (jax.nn.sigmoid(logits) - diag)).astype(bf16)
        coef_out[part] = coef
        total = total + lax.dot_general(
            coef, txt[part], (((0,), (0,)), ((), ())), preferred_element_type=f32
        )
    terms[...] = total
    half = nz * own
    for k, by in enumerate(ahead):
        owner = lax.rem(z + by, nz) * own
        near = pl.multiple_of(core * half + owner, own)
        far = pl.multiple_of((1 - core) * half + owner, own)
        near_out[pl.ds(k * own, own)] = terms[pl.ds(near, own)]
        far_out[pl.ds(k * own, own)] = terms[pl.ds(far, own)].astype(bf16)


def image_terms(own, log_temp, bias, factor, img, txt):
    m, w = txt.shape
    i = img.shape[0]
    return pl.pallas_call(
        functools.partial(image_kernel, own, factor),
        out_shape=[
            jax.ShapeDtypeStruct((m, i), bf16),
            jax.ShapeDtypeStruct((i // 2, w), f32),
            jax.ShapeDtypeStruct((i // 2, w), bf16),
        ],
        in_specs=[smem, smem, vmem, vmem],
        out_specs=[vmem, vmem, vmem],
        scratch_shapes=[pltpu.VMEM((i, w), f32)],
        cost_estimate=cost(4 * i * m * w, 4 * (i + m) * w, i * m),
        compiler_params=params,
    )(log_temp, bias, img, txt)


def text_kernel(coef, img, out, buf, sems):
    rows = img[...]
    parts, size = buf.shape[:2]
    writes = []
    for q in range(parts):
        buf[q] = jnp.dot(
            coef[q * size : (q + 1) * size], rows, preferred_element_type=f32
        ).astype(bf16)
        writes.append(pltpu.make_async_copy(buf.at[q], out.at[pl.ds(q * size, size)], sems.at[q]))
        writes[-1].start()
    for write in writes:
        write.wait()


def text_terms(coef, img):
    m, i = coef.shape
    w = img.shape[1]
    parts = 2
    return pl.pallas_call(
        text_kernel,
        out_shape=pltpu.HBM((m, w), bf16),
        in_specs=[vmem, vmem],
        out_specs=hbm,
        scratch_shapes=[
            pltpu.VMEM((parts, m // parts, w), bf16),
            pltpu.SemaphoreType.DMA((parts,)),
        ],
        cost_estimate=cost(2 * i * m * w, 4 * (i + m) * w),
        compiler_params=params,
    )(coef, img)


def fold_kernel(n, *refs):
    parts, outs = refs[:n], refs[n:]
    at = 0
    for out in outs:
        rows = slice(at, at + out.shape[0])
        total = parts[0][rows]
        for part in parts[1:]:
            total = total + part[rows].astype(f32)
        out[...] = total.astype(out.dtype)
        at += out.shape[0]


def fold(size, *parts):
    n, w = parts[0].shape
    work = 10**10
    return pl.pallas_call(
        functools.partial(fold_kernel, len(parts)),
        out_shape=[
            jax.ShapeDtypeStruct((size, w), f32 if k == 0 else bf16) for k in range(n // size)
        ],
        in_specs=[vmem] * len(parts),
        out_specs=[vmem] * (n // size),
        cost_estimate=cost(work, 10 * n * w),
        compiler_params=params,
    )(*parts)


def backprop_kernel(ahead_of, unit, inv, proj, *refs):
    if ahead_of:
        following, *refs = refs
    *refs, unit_buf, proj_buf, sems = refs
    cuts, cut = proj_buf.shape[:2]
    reads = [pltpu.make_async_copy(unit, unit_buf, sems.at[cuts])]
    for k in range(cuts):
        reads.append(pltpu.make_async_copy(proj.at[pl.ds(k * cut, cut)], proj_buf.at[k], sems.at[k]))
    if ahead_of:
        *refs, following_out = refs
        reads.append(pltpu.make_async_copy(following, following_out, sems.at[cuts + 1]))
    *parts, out = refs
    for read in reads:
        read.start()
    total = 0.0
    for part in parts:
        if len(part.shape) == 2:
            total = total + part[...].astype(f32)
        else:
            for k in range(part.shape[0]):
                total = total + part[k].astype(f32)
    reads[0].wait()
    rows = unit_buf[...]
    along = jnp.sum(rows * total, axis=1, keepdims=True)
    delta = (inv[:, :1] * (total - rows * along)).astype(bf16)
    for k in range(cuts):
        reads[k + 1].wait()
        out[:, k * cut : (k + 1) * cut] = lax.dot_general(
            delta, proj_buf[k], (((1,), (1,)), ((), ())), preferred_element_type=f32
        )
    if ahead_of:
        reads[-1].wait()


def backprop(unit, inv, proj, parts, following=None):
    depth, width = proj.shape
    own = unit.shape[0]
    cut = 512
    more = following is not None
    outs = [jax.ShapeDtypeStruct((own, depth), f32)]
    if more:
        outs.append(jax.ShapeDtypeStruct(following.shape, bf16))
    return pl.pallas_call(
        functools.partial(backprop_kernel, more),
        out_shape=outs,
        in_specs=[hbm, vmem, hbm] + [hbm] * more + [vmem] * len(parts),
        out_specs=[vmem] * len(outs),
        scratch_shapes=[
            pltpu.VMEM(unit.shape, f32),
            pltpu.VMEM((depth // cut, cut, width), bf16),
            pltpu.SemaphoreType.DMA((depth // cut + 2,)),
        ],
        cost_estimate=cost(2 * own * depth * width, 2 * depth * width),
        compiler_params=params,
    )(far_off(unit), inv, far_off(proj), *([far_off(following)] * more), *parts)


def last_kernel(unit, inv, proj, parts, out):
    total = parts[0].astype(f32)
    for k in range(1, parts.shape[0]):
        total += parts[k].astype(f32)
    rows = unit[...]
    along = jnp.sum(rows * total, axis=1, keepdims=True)
    delta = (inv[:, :1] * (total - rows * along)).astype(bf16)
    out[...] = lax.dot_general(
        delta, proj[...], (((1,), (1,)), ((), ())), preferred_element_type=f32
    )


def last_backprop(unit, inv, proj, parts):
    depth, width = proj.shape
    own = unit.shape[0]
    return pl.pallas_call(
        last_kernel,
        out_shape=jax.ShapeDtypeStruct((own, depth), f32),
        in_specs=[vmem] * 4,
        out_specs=vmem,
        cost_estimate=cost(2 * own * depth * width, 2 * depth * width),
        compiler_params=params,
    )(far_off(unit), inv, proj, parts)


def shards(image_feats, text_feats, image_proj, text_proj, log_temp, logit_bias):
    own = text_feats.shape[0]
    total = own * lax.axis_size(("y", "x", "core", "z"))
    send = lambda rows, axis, by: lax.ppermute(rows, axis, shift(axis, by))

    copies = lax.axis_size(("y", "x"))
    txt_unit, txt_inv, txt_rows, img_unit, img_inv, img_rows = embed(
        text_feats, text_proj, image_feats, image_proj, copies
    )
    txt_rows = exchanged(txt_rows, ("y", "x")).reshape(-1, txt_rows.shape[2])
    img_rows = lax.all_gather(img_rows, "z", tiled=True)
    img_rows = lax.all_gather(img_rows, "core", tiled=True)

    coef, near, far = image_terms(
        own, log_temp, logit_bias, loss_scale / total, img_rows, txt_rows
    )
    far = send(far, "core", 1)
    txt_terms = text_terms(coef, img_rows)
    txt_terms = exchanged(txt_terms.reshape(-1, own, txt_terms.shape[1]), ("y", "x"))
    near, by1, by2, back = fold(3 * own, near, far)
    near, by4, by8 = fold(
        own, near, send(by1, "z", 1), send(by2, "z", 2), send(back, "z", -1)
    )
    parts = (near, send(by4, "z", 4), send(by8, "z", 8))
    image_grad, weights = backprop(img_unit, img_inv, image_proj, parts, text_proj)
    text_grad = last_backprop(txt_unit, txt_inv, weights, txt_terms)
    return (image_grad, text_grad)


def solution(mesh):
    blk, grp = mesh.devices.shape
    fine = Mesh(np.asarray(mesh.devices).reshape(blk // 8, 4, 2, grp), ("y", "x", "core", "z"))
    rows = P(("y", "x", "core", "z"), None)
    return jax.shard_map(
        shards,
        mesh=fine,
        in_specs=(rows, rows, P(), P(), P(), P()),
        out_specs=(rows, rows),
        check_vma=False,
    )
```
